256 devices in a mesh: dp: 16 (over x_lo, z), expert: 16 (over y, x_hi, core).
Axes of the slice: x: 4 (x_hi: 2, x_lo: 2; x = x_hi * 2 + x_lo), y: 4, z: 8, core: 2. Of those that a mesh axis runs over, the one named last changes fastest.
Arguments:
- query: bfloat16 [32768, 4096], P(('dp', 'expert')), may hold values from -6 to 6
- key: bfloat16 [32768, 4096], P(('dp', 'expert')), may hold values from -6 to 6
- value: bfloat16 [32768, 4096], P(('dp', 'expert')), may hold values from -6 to 6
- resid: bfloat16 [32768, 4096], P(('dp', 'expert')), may hold values from -6 to 6
- d_out: bfloat16 [32768, 4096], P(('dp', 'expert')), may hold values from -6 to 6
- routes: int32 [32768, 2], P(('dp', 'expert')), may hold values from 0 to 63, as said below
- gates: float32 [32768, 2], P(('dp', 'expert')), may hold values from 0.2 to 1
- w_up: bfloat16 [4096, 16384], P('dp', 'expert'), may hold values from -0.09375 to 0.09375
- w_down: bfloat16 [4096, 16384], P('dp', 'expert'), may hold values from -0.046875 to 0.046875
Outputs:
- grad_query: bfloat16 [32768, 4096], P(('dp', 'expert'))
- grad_key: bfloat16 [32768, 4096], P(('dp', 'expert'))
- grad_value: bfloat16 [32768, 4096], P(('dp', 'expert'))
- grad_up: bfloat16 [4096, 16384], P('dp', 'expert')
- grad_down: bfloat16 [4096, 16384], P('dp', 'expert')
The draws below stay inside these ranges and needn't reach their ends.
Inputs may be any that keep to these rules, and one draw needn't show every extreme that they name: `routes`: the two experts of a token differ. Among the tokens of one device (aligned blocks of 128 rows) between 1 and 4 name expert 0, and some device has exactly 4.
All inputs are finite; a program needn't handle non-finite values.
Results may differ from the reference program's by a relative error of at most 0.011.
The reference program's roundings to bfloat16 on the way count: a program that leaves them out, or rounds other values in their place, can miss the bound.
Values may be sent and summed in bfloat16 or wider, within the bound.
A program may use at most 128 MiB of HBM per device.

```python
from functools import partial
import jax
import jax.numpy as jnp
from jax import lax

D = 4096
FF = 16384
HEADS = 64
HEAD = 64
EXPERTS_ALL = 64
CAP = 4
TOK_DEV = 128
TOKENS = 32768
DEVICES = 256


def draw_query(key, part):
    own_key = jax.random.fold_in(key, 21)
    return jnp.clip(jax.random.normal(own_key, (TOKENS, D), jnp.float32), -6.0, 6.0).astype(jnp.bfloat16)


def draw_key(key, part):
    own_key = jax.random.fold_in(key, 22)
    return jnp.clip(jax.random.normal(own_key, (TOKENS, D), jnp.float32), -6.0, 6.0).astype(jnp.bfloat16)


def draw_routes(key, part):
    key = jax.random.fold_in(key, 11)
    key_list = jax.random.split(key, 6)
    blocks = TOKENS // TOK_DEV
    first_pick = jax.random.randint(key_list[0], (TOKENS,), 1, EXPERTS_ALL)
    offset_pick = jax.random.randint(key_list[1], (TOKENS,), 1, EXPERTS_ALL - 1)
    second = 1 + (first_pick - 1 + offset_pick) % (EXPERTS_ALL - 1)
    block_loads = jax.random.randint(key_list[2], (blocks,), 1, CAP + 1)
    fullest = jax.random.randint(key_list[3], (), 0, blocks)
    block_loads = jnp.where(jnp.arange(blocks) == fullest, CAP, block_loads)
    orders = jax.vmap(lambda subkey: jax.random.permutation(subkey, TOK_DEV))(jax.random.split(key_list[4], blocks))
    token_rank = jnp.argsort(orders, axis=1)
    chosen = (token_rank < block_loads[:, None]).reshape(TOKENS)
    column = jax.random.randint(key_list[5], (TOKENS,), 0, 2)
    first_route = jnp.where(chosen & (column == 0), 0, first_pick)
    second_route = jnp.where(chosen & (column == 1), 0, second)
    return jnp.stack([first_route, second_route], axis=1).astype(jnp.int32)


def block_scale(key, extent, cuts, smallest, top_value):
    gain = 1.0
    for dim, parts in cuts:
        heights = jax.random.uniform(jax.random.fold_in(jax.random.fold_in(key, 6), dim), (parts,), jnp.float32, smallest / len(cuts), top_value / len(cuts))
        gain = gain * jnp.repeat(jnp.exp(heights), extent[dim] // parts).reshape((-1,) + (1,) * (len(extent) - 1 - dim))
    return gain


def normal_values(rng, shape, scale, limit, cuts=(), kind=jnp.bfloat16):
    drawn = jax.random.normal(rng, shape, jnp.float32) * scale
    if len(cuts) > 0:
        drawn = block_scale(rng, shape, cuts, -0.22, 0.18) * drawn
    return jnp.clip(drawn, min=-limit, max=limit).astype(kind)


def setup_inputs(seed: int = 0) -> dict:
    arg_keys = jax.random.split(jax.random.key(seed), 10)
    query = draw_query(jax.random.fold_in(arg_keys[9], 71), 0)
    key = draw_key(jax.random.fold_in(arg_keys[9], 71), 0)
    value = normal_values(arg_keys[2], (TOKENS, D), 1.0, 6.0, ((0, 256),))
    resid = normal_values(arg_keys[3], (TOKENS, D), 1.0, 6.0, ((0, 256),))
    d_out = normal_values(arg_keys[4], (TOKENS, D), 1.0, 6.0, ((0, 256),))
    routes = draw_routes(jax.random.fold_in(arg_keys[9], 71), 0)
    gates = jnp.clip(0.2 + 0.8 * jax.random.uniform(arg_keys[6], (TOKENS, 2), jnp.float32) ** block_scale(arg_keys[6], (TOKENS, 2), ((0, 256),), -0.2, 0.2), 0.2, 1.0)
    w_up = normal_values(arg_keys[7], (D, FF), D ** -0.5, 0.09375, ((0, 16), (1, 16)))
    w_down = normal_values(arg_keys[8], (D, FF), FF ** -0.5, 0.046875, ((0, 16), (1, 16)))
    return {"query": query, "key": key, "value": value, "resid": resid, "d_out": d_out, "routes": routes, "gates": gates, "w_up": w_up, "w_down": w_down}


EPS = 1e-06

def activate(hidden):
    outputs, pullback = jax.vjp(partial(jax.nn.gelu, approximate=True), hidden)
    return (outputs, pullback(jnp.ones_like(hidden))[0])

def attend_forward(query, key, value):
    length = query.shape[0]
    scaling = HEAD ** (-0.5)
    query_heads = query.astype(jnp.float32).reshape(length, HEADS, HEAD)
    key_heads = key.astype(jnp.float32).reshape(length, HEADS, HEAD)
    value_heads = value.astype(jnp.float32).reshape(length, HEADS, HEAD)
    scores = jnp.einsum('shd,thd->hst', query_heads, key_heads) * scaling
    causal = jnp.arange(length)[:, None] >= jnp.arange(length)[None, :]
    scores = jnp.where(causal[None], scores, -jnp.inf)
    row_peak = lax.optimization_barrier(jnp.max(scores, axis=-1, keepdims=True))
    weights = jnp.exp(scores - row_peak)
    probability = weights / lax.optimization_barrier(jnp.sum(weights, axis=-1, keepdims=True))
    rounded = probability.astype(jnp.bfloat16)
    mixture = jnp.einsum('hst,thd->shd', rounded.astype(jnp.float32), value_heads)
    return (probability, rounded, mixture.reshape(length, HEADS * HEAD))

def attend_backward(query, key, value, upstream):
    length = query.shape[0]
    scaling = HEAD ** (-0.5)
    probability, rounded, mixture = attend_forward(query, key, value)
    query_heads = query.astype(jnp.float32).reshape(length, HEADS, HEAD)
    key_heads = key.astype(jnp.float32).reshape(length, HEADS, HEAD)
    value_heads = value.astype(jnp.float32).reshape(length, HEADS, HEAD)
    grad_heads = upstream.astype(jnp.float32).reshape(length, HEADS, HEAD)
    value_grad = jnp.einsum('hst,shd->thd', rounded.astype(jnp.float32), grad_heads)
    prob_grad = jnp.einsum('shd,thd->hst', grad_heads, value_heads)
    row_delta = lax.optimization_barrier(jnp.sum(grad_heads * mixture.reshape(length, HEADS, HEAD), axis=-1)).T
    score_grad = (probability * (prob_grad - row_delta[:, :, None])).astype(jnp.bfloat16)
    score_wide = score_grad.astype(jnp.float32)
    query_grad = jnp.einsum('hst,thd->shd', score_wide, key_heads) * scaling
    key_grad = jnp.einsum('hst,shd->thd', score_wide, query_heads) * scaling
    shape_out = (length, HEADS * HEAD)
    return (query_grad.reshape(shape_out).astype(jnp.bfloat16), key_grad.reshape(shape_out).astype(jnp.bfloat16), value_grad.reshape(shape_out).astype(jnp.bfloat16))

def reference(query, key, value, resid, d_out, routes, gates, w_up, w_down):
    per_seq = (TOKENS // TOK_DEV, TOK_DEV, D)
    mixture = lax.map(lambda pieces: attend_forward(*pieces)[2], (query.reshape(per_seq), key.reshape(per_seq), value.reshape(per_seq)))
    state = resid.astype(jnp.float32) + mixture.reshape(TOKENS, D)
    root_mean = jnp.sqrt(lax.optimization_barrier(jnp.mean(state * state, axis=-1, keepdims=True)) + EPS)
    normed = state / root_mean
    normed_input = normed.astype(jnp.bfloat16)
    upstream = d_out.astype(jnp.float32)
    chosen = routes == 0
    has_route = jnp.any(chosen, axis=1)
    picked_gate = lax.optimization_barrier(jnp.sum(jnp.where(chosen, gates, jnp.zeros_like(gates)), axis=1))
    out_grad = (picked_gate[:, None] * upstream).astype(jnp.bfloat16)
    hit_table = has_route.reshape(DEVICES, TOK_DEV).astype(jnp.int32)
    slot_index = (jnp.cumsum(hit_table, axis=1) - 1).astype(jnp.int32)
    row_total = DEVICES * CAP
    base = jnp.arange(DEVICES, dtype=jnp.int32)[:, None] * CAP
    position = jnp.where(hit_table > 0, base + slot_index, row_total).reshape(-1).astype(jnp.int32)
    empty_rows = jnp.zeros((row_total + 1, D), jnp.bfloat16)
    rows_input = empty_rows.at[position].set(normed_input)[:row_total]
    rows_grad = empty_rows.at[position].set(out_grad)[:row_total]
    hidden = jnp.dot(rows_input, w_up, preferred_element_type=jnp.float32)
    activation, gradient_slope = activate(hidden)
    activation = activation.astype(jnp.bfloat16)
    back_grad = jnp.dot(rows_grad, w_down, preferred_element_type=jnp.float32)
    hidden_grad = (back_grad * gradient_slope).astype(jnp.bfloat16)
    returned = lax.dot_general(hidden_grad, w_up, (((1,), (1,)), ((), ())), preferred_element_type=jnp.float32).astype(jnp.bfloat16)
    grad_up = lax.dot_general(rows_input, hidden_grad, (((0,), (0,)), ((), ())), preferred_element_type=jnp.float32).astype(jnp.bfloat16)
    grad_down = lax.dot_general(rows_grad, activation, (((0,), (0,)), ((), ())), preferred_element_type=jnp.float32).astype(jnp.bfloat16)
    padded = jnp.concatenate([returned, jnp.zeros((1, D), jnp.bfloat16)], axis=0)
    normed_grad = padded[position].astype(jnp.float32)
    state_grad = upstream + (normed_grad - normed * lax.optimization_barrier(jnp.mean(normed_grad * normed, axis=-1, keepdims=True))) / root_mean
    state_grad = state_grad.astype(jnp.bfloat16)
    grad_parts = lax.map(lambda pieces: attend_backward(*pieces), (query.reshape(per_seq), key.reshape(per_seq), value.reshape(per_seq), state_grad.reshape(per_seq)))
    grad_query, grad_key, grad_value = [piece.reshape(TOKENS, D) for piece in grad_parts]
    return (grad_query, grad_key, grad_value, grad_up, grad_down)
```

```python
import functools

import jax
import jax.numpy as jnp
from jax import lax
from jax.experimental import pallas as pl
from jax.experimental.pallas import tpu as pltpu
from jax.sharding import PartitionSpec as P

MESH = pl.DeviceIdType.MESH
F32 = jnp.float32
BF16 = jnp.bfloat16
D = 4096
SCALE = 0.125
EPS = 1e-06
Y_OFFSETS = (0, 1, 3, 2)
PAIRS = 32


def dot(a, b):
    return lax.dot_general(a, b, (((1,), (0,)), ((), ())), preferred_element_type=F32)


def dot_t(a, b):
    return lax.dot_general(a, b, (((1,), (1,)), ((), ())), preferred_element_type=F32)


def t_dot(a, b):
    return lax.dot_general(a, b, (((0,), (0,)), ((), ())), preferred_element_type=F32)


def iota(shape, dim):
    return lax.broadcasted_iota(jnp.int32, shape, dim)


def kernel(
    aux_ref, q_hbm, k_hbm, v_hbm, r_hbm, d_hbm, wu_hbm, wd_hbm,
    dq_hbm, dk_hbm, dv_hbm, gu_hbm, gd_hbm,
    q, k, v, r, d, wu, wd, keep, qr, dlo, state, prob,
    asend, arecv, g, part, rsp, rsm, ag, gu_acc, gd_acc, gu_out, gd_out,
    rsend, rcore, rysend, ryrecv, rxsend, rxrecv, hsend, hrecv,
    dq, dkb, dvb, dko, dvo,
    load_sem, out_sem, w_send, w_recv, a_send, a_recv, x_send, x_recv, c_send, c_recv, y_send, y_recv,
    rs_send, rs_recv, ag_send, ag_recv, rc_send, rc_recv, ry_send, ry_recv, rx_send, rx_recv, h_send, h_recv,
    o_send, o_recv,
):
    i = lax.axis_index("dp")
    j = lax.axis_index("expert")
    xl = i // 8
    z = i % 8
    y = j // 4
    xh = (j // 2) % 2
    c = j % 2
    x = xh * 2 + xl

    def dev(x_to, y_to, z_to, c_to):
        return ((x_to % 2) * 8 + z_to, y_to * 4 + (x_to // 2) * 2 + c_to)

    def z_peer(step):
        return dev(x, y, (z + step) % 8, c)

    def x_peer(step):
        return dev((x + step) % 4, y, z, c)

    def y_peer(step):
        return dev(x, (y + step) % 4, z, c)

    core_peer = dev(x, y, z, 1 - c)
    pair_peer = (((1 - xl) * 8 + z), j)

    barrier = pltpu.get_barrier_semaphore()
    peers = [z_peer(s) for s in range(1, 8)] + [x_peer(s) for s in range(1, 4)]
    peers += [y_peer(s) for s in range(1, 4)] + [core_peer]
    for peer in peers:
        pl.semaphore_signal(barrier, inc=1, device_id=peer, device_id_type=MESH)

    loads = []
    for n, (src, dst) in enumerate(((q_hbm, q), (k_hbm, k), (v_hbm, v), (r_hbm, r), (d_hbm, d))):
        loads.append(pltpu.make_async_copy(src, dst, load_sem.at[n]))
    own_cols = pl.ds(pl.multiple_of(xl * 512, 512), 512)
    other_cols = pl.ds(pl.multiple_of((1 - xl) * 512, 512), 512)
    loads.append(pltpu.make_async_copy(wd_hbm.at[:, own_cols], wd.at[xl], load_sem.at[5]))
    loads.append(pltpu.make_async_copy(wu_hbm.at[:, own_cols], wu.at[xl], load_sem.at[6]))
    for copy in loads:
        copy.start()

    pl.semaphore_wait(barrier, len(peers))

    sent = []

    def send(src, dst, send_sem, recv_sem, peer):
        copy = pltpu.make_async_remote_copy(
            src_ref=src, dst_ref=dst, send_sem=send_sem, recv_sem=recv_sem, device_id=peer, device_id_type=MESH
        )
        copy.start()
        sent.append(copy)

    def arrived(dst, send_sem, recv_sem, peer):
        pltpu.make_async_remote_copy(
            src_ref=dst, dst_ref=dst, send_sem=send_sem, recv_sem=recv_sem, device_id=peer, device_id_type=MESH
        ).wait_recv()

    send(wd_hbm.at[:, other_cols], wd.at[xl], w_send.at[0], w_recv.at[0], pair_peer)
    send(wu_hbm.at[:, other_cols], wu.at[xl], w_send.at[1], w_recv.at[1], pair_peer)

    flags = aux_ref[0:2, :]
    gate_row = aux_ref[2:3, :] * flags[0:1, :] + aux_ref[3:4, :] * flags[1:2, :]
    hit = jnp.maximum(flags[0:1, :], flags[1:2, :])
    upper = (iota((128, 128), 0) <= iota((128, 128), 1)).astype(BF16)
    hits = jnp.broadcast_to(hit, (8, 128))
    rank = dot(hits.astype(BF16), upper) - 1.0
    slot = iota((8, 128), 0).astype(F32)
    sel = jnp.where((rank == slot) & (slot < 4.0), hits, 0.0)
    sel_hi = jnp.where(rank == slot - 4.0, hits, 0.0)
    occupied = jnp.sum(sel, axis=1, keepdims=True)
    position = jnp.sum(sel * iota((8, 128), 1).astype(F32), axis=1, keepdims=True)
    gate_hi = jnp.sum(sel_hi * gate_row, axis=1, keepdims=True)
    sel_b = sel.astype(BF16)
    sel_both = jnp.concatenate([sel, sel_hi], axis=0).astype(BF16)
    keep[...] = (1.0 - t_dot(sel_b, jnp.ones((8, 128), BF16))).astype(BF16)
    seen = iota((8, 128), 1).astype(F32) <= position
    seen32 = jnp.concatenate([seen.astype(F32)] * 4, axis=0) > 0.5
    lane_head = iota((8, 256), 1) // 64

    def spread(rows):
        return jnp.concatenate([jnp.where(lane_head == h, rows, 0.0) for h in range(4)], axis=0).astype(BF16)

    def fold(rows):
        total = jnp.where(lane_head == 0, rows[0:8], 0.0)
        for h in range(1, 4):
            total = total + jnp.where(lane_head == h, rows[8 * h : 8 * h + 8], 0.0)
        return total

    for copy in loads[:5]:
        copy.wait()

    def routed_forward(n, squares):
        cols = pl.ds(pl.multiple_of(n * 256, 256), 256)
        q_rows = dot(sel_b, q[:, cols]) * SCALE
        qr[:, cols] = q_rows
        scores = jnp.where(seen32, dot_t(spread(q_rows), k[:, cols]), -jnp.inf)
        weights = jnp.exp(scores - jnp.max(scores, axis=1, keepdims=True))
        p = weights / jnp.sum(weights, axis=1, keepdims=True)
        prob[n] = p
        mixture = fold(dot(p.astype(BF16), v[:, cols]))
        st = dot(sel_b, r[:, cols]) + mixture
        state[:, cols] = st
        d_rows = dot(sel_both, d[:, cols])
        dlo[:, cols] = d_rows
        return squares + jnp.sum(st * st, axis=1, keepdims=True)

    squares = jnp.zeros((8, 1), F32)
    squares = lax.fori_loop(0, 16, routed_forward, squares, unroll=4)
    root_mean = jnp.sqrt(squares / D + EPS)
    low_row = iota((8, 256), 0) < 4

    def slot_rows(n):
        cols = slice(n * 256, n * 256 + 256)
        normed = state[:, cols] / root_mean * occupied
        return jnp.where(low_row, normed, gate_hi * dlo[8:16, cols])

    for n in range(8):
        asend[n] = jnp.concatenate([slot_rows(n), slot_rows(8 + n)], axis=0).astype(BF16)
    for s in range(1, 8):
        send(asend.at[(z + s) % 8], arecv.at[z], a_send.at[s - 1], a_recv.at[s - 1], z_peer(s))
    arecv[z] = asend[z]

    lane0 = iota((128, 128), 1) < 64
    causal = iota((256, 128), 0) % 128 >= iota((256, 128), 1)

    def two(rows):
        zero = jnp.zeros_like(rows)
        return jnp.concatenate([jnp.where(lane0, rows, zero), jnp.where(lane0, zero, rows)], axis=0)

    def attend(n, carry):
        cols = pl.ds(pl.multiple_of(n * 128, 128), 128)
        k2 = k[:, cols]
        qs = two(q[:, cols] * jnp.asarray(SCALE, BF16))
        scores = jnp.where(causal, dot_t(qs, k2), -jnp.inf)
        weights = jnp.exp(scores - jnp.max(scores, axis=1, keepdims=True))
        p = weights / jnp.sum(weights, axis=1, keepdims=True)
        pb = p.astype(BF16)
        ds = two(d[:, cols] * keep[...])
        dp = dot_t(ds, v[:, cols])
        delta = jnp.sum(pb.astype(F32) * dp, axis=1, keepdims=True)
        sg = (p * (dp - delta)).astype(BF16)
        dkb[:, cols] = t_dot(sg, qs)
        dvb[:, cols] = t_dot(pb, ds)
        sides = jnp.concatenate([sg[:128], sg[128:]], axis=1)
        dq[:, cols] = (dot(sides, two(k2)) * SCALE).astype(BF16)
        return carry

    done_pairs = [0]

    def attend_some(count):
        first = done_pairs[0]
        last = min(PAIRS, first + count)
        if last > first:
            lax.fori_loop(first, last, attend, 0)
        done_pairs[0] = last

    attend_some(4)

    for s in range(1, 8):
        arrived(arecv.at[(z + 8 - s) % 8], a_send.at[s - 1], a_recv.at[s - 1], z_peer(s))
    row = iota((128, 128), 0)
    col = iota((128, 128), 1)
    permute = ((row // 32 == (col // 4) % 4) & ((row % 32) // 4 == col // 16) & (row % 4 == col % 4)).astype(BF16)
    tiles = dot(permute, arecv[...].reshape(128, 256)).astype(BF16)
    g[y, c, x] = tiles.reshape(4, 32, 256)
    for s in range(1, 4):
        send(g.at[y, c, x], g.at[y, c, x], x_send.at[s - 1], x_recv.at[s - 1], x_peer(s))
    attend_some(2)
    for s in range(1, 4):
        arrived(g.at[y, c, (x + 4 - s) % 4], x_send.at[s - 1], x_recv.at[s - 1], x_peer(s))
    send(g.at[y, c], g.at[y, c], c_send.at[0], c_recv.at[0], core_peer)
    for w in range(1, 4):
        send(g.at[y, c], g.at[y, c], y_send.at[w - 1], y_recv.at[w - 1], y_peer(4 - Y_OFFSETS[w]))
    for copy in loads[5:]:
        copy.wait()
    arrived(wd.at[1 - xl], w_send.at[0], w_recv.at[0], pair_peer)
    arrived(wu.at[1 - xl], w_send.at[1], w_recv.at[1], pair_peer)

    def y_of(w):
        return (y + Y_OFFSETS[w]) % 4

    def rows_of(w, f, m):
        return g[y_of(w), :, :, f * 2 + m].reshape(256, 256)

    def gather(w):
        if w > 0:
            arrived(g.at[y_of(w), c], y_send.at[w - 1], y_recv.at[w - 1], y_peer(1))
            send(g.at[y_of(w), c], g.at[y_of(w), c], c_send.at[w], c_recv.at[w], core_peer)

    up_half = slice(0, 16)
    down_half = slice(16, 32)

    def reduce_start(w):
        arrived(g.at[y_of(w), 1 - c], c_send.at[w], c_recv.at[w], core_peer)
        hidden = dot(rows_of(w, 0, 0), wu[0]) + dot(rows_of(w, 1, 0), wu[1])
        part[w, :, :, 0:512] = hidden.astype(BF16).reshape(8, 32, 512)
        back = dot(rows_of(w, 0, 1), wd[0]) + dot(rows_of(w, 1, 1), wd[1])
        part[w, :, :, 512:1024] = back.astype(BF16).reshape(8, 32, 512)
        far = (z + 4) % 8
        send(part.at[w, far, up_half], rsp.at[w, 0, up_half], rs_send.at[w, 0], rs_recv.at[w, 0], z_peer(1))
        send(part.at[w, far, down_half], rsm.at[w, 0, down_half], rs_send.at[w, 4], rs_recv.at[w, 4], z_peer(7))

    def add(buf, w, s, rows, block):
        buf[w, s, rows] = (buf[w, s, rows].astype(F32) + part[w, block, rows].astype(F32)).astype(BF16)

    def reduce_step(w, s):
        up = (z + 4 - s) % 8
        down = (z + 4 + s) % 8
        if s == 1:
            arrived(rsp.at[w, 0, up_half], rs_send.at[w, 0], rs_recv.at[w, 0], z_peer(1))
            add(rsp, w, 0, up_half, up)
            rsp[w, 0, down_half] = part[w, up, down_half]
        else:
            arrived(rsp.at[w, s - 1], rs_send.at[w, s - 1], rs_recv.at[w, s - 1], z_peer(1))
            add(rsp, w, s - 1, slice(0, 32), up)
        send(rsp.at[w, s - 1], rsp.at[w, s], rs_send.at[w, s], rs_recv.at[w, s], z_peer(1))
        if s == 1:
            arrived(rsm.at[w, 0, down_half], rs_send.at[w, 4], rs_recv.at[w, 4], z_peer(7))
            add(rsm, w, 0, down_half, down)
            rsm[w, 0, up_half] = part[w, down, up_half]
        else:
            arrived(rsm.at[w, s - 1], rs_send.at[w, 3 + s], rs_recv.at[w, 3 + s], z_peer(7))
            add(rsm, w, s - 1, slice(0, 32), down)
        send(rsm.at[w, s - 1], rsm.at[w, s], rs_send.at[w, 4 + s], rs_recv.at[w, 4 + s], z_peer(7))

    def activate(w):
        arrived(rsp.at[w, 3], rs_send.at[w, 3], rs_recv.at[w, 3], z_peer(1))
        arrived(rsm.at[w, 3], rs_send.at[w, 7], rs_recv.at[w, 7], z_peer(7))
        total = part[w, z].astype(F32) + rsp[w, 3].astype(F32) + rsm[w, 3].astype(F32)
        h = total[:, 0:512]
        root = 0.7978845608028654
        inner = jnp.tanh(root * (h + 0.044715 * (h * h * h)))
        half = 0.5 * (1.0 + inner)
        slope = half + 0.5 * h * (1.0 - inner * inner) * (root * (1.0 + 3.0 * 0.044715 * (h * h)))
        ag[w, z, :, 0:512] = (total[:, 512:1024] * slope).astype(BF16)
        ag[w, z, :, 512:1024] = (h * half).astype(BF16)
        send(ag.at[w, z], ag.at[w, z], ag_send.at[w, 0], ag_recv.at[w, 0], z_peer(1))
        send(ag.at[w, z], ag.at[w, z], ag_send.at[w, 4], ag_recv.at[w, 4], z_peer(7))

    def forward(w, s):
        up = (z + 8 - s) % 8
        down = (z + s) % 8
        arrived(ag.at[w, up], ag_send.at[w, s - 1], ag_recv.at[w, s - 1], z_peer(1))
        rows = up_half if s == 3 else slice(0, 32)
        send(ag.at[w, up, rows], ag.at[w, up, rows], ag_send.at[w, s], ag_recv.at[w, s], z_peer(1))
        arrived(ag.at[w, down], ag_send.at[w, 3 + s], ag_recv.at[w, 3 + s], z_peer(7))
        rows = down_half if s == 3 else slice(0, 32)
        send(ag.at[w, down, rows], ag.at[w, down, rows], ag_send.at[w, 4 + s], ag_recv.at[w, 4 + s], z_peer(7))

    def gradients(w):
        far = (z + 4) % 8
        arrived(ag.at[w, far, up_half], ag_send.at[w, 3], ag_recv.at[w, 3], z_peer(1))
        arrived(ag.at[w, far, down_half], ag_send.at[w, 7], ag_recv.at[w, 7], z_peer(7))
        hidden_grad = ag[w, :, :, 0:512].reshape(256, 512)
        for f in range(2):
            back = dot_t(hidden_grad, wu[f]).astype(BF16)
            rsend[w, :, :, f * 256 : f * 256 + 256] = back.reshape(2, 128, 256)
        send(rsend.at[w, 1 - c], rcore.at[w], rc_send.at[w], rc_recv.at[w], core_peer)
        activation = ag[w, :, :, 512:1024].reshape(256, 512)
        for f in range(2):
            up = t_dot(rows_of(w, f, 0), hidden_grad)
            down = t_dot(rows_of(w, f, 1), activation)
            if w == 0:
                gu_acc[f] = up
                gd_acc[f] = down
            elif w < 3:
                gu_acc[f] += up
                gd_acc[f] += down
            else:
                gu_out[f] = (gu_acc[f] + up).astype(BF16)
                gd_out[f] = (gd_acc[f] + down).astype(BF16)

    def give_back(w):
        arrived(rcore.at[w], rc_send.at[w], rc_recv.at[w], core_peer)
        total = rsend[w, c].astype(F32) + rcore[w].astype(F32)
        rysend[w] = total.astype(BF16)
        if w > 0:
            send(rysend.at[w], ryrecv.at[w - 1], ry_send.at[w - 1], ry_recv.at[w - 1], y_peer(Y_OFFSETS[w]))

    stages = [
        lambda w: gather(w),
        lambda w: reduce_start(w),
        lambda w: reduce_step(w, 1),
        lambda w: reduce_step(w, 2),
        lambda w: reduce_step(w, 3),
        lambda w: activate(w),
        lambda w: forward(w, 1),
        lambda w: forward(w, 2),
        lambda w: forward(w, 3),
        lambda w: gradients(w),
        lambda w: give_back(w),
    ]
    spacing = 2
    for tick in range(len(stages) + 3 * spacing):
        for w in range(4):
            stage = tick - spacing * w
            if 0 <= stage < len(stages):
                stages[stage](w)
        attend_some(2)
    attend_some(PAIRS)

    send(gu_out.at[1 - xl], gu_hbm.at[:, own_cols], o_send.at[0], o_recv.at[0], pair_peer)
    send(gd_out.at[1 - xl], gd_hbm.at[:, own_cols], o_send.at[1], o_recv.at[1], pair_peer)
    outs = [
        pltpu.make_async_copy(gu_out.at[xl], gu_hbm.at[:, own_cols], out_sem.at[0]),
        pltpu.make_async_copy(gd_out.at[xl], gd_hbm.at[:, own_cols], out_sem.at[1]),
    ]
    for copy in outs:
        copy.start()

    total = rysend[0].astype(F32)
    for w in range(1, 4):
        arrived(ryrecv.at[w - 1], ry_send.at[w - 1], ry_recv.at[w - 1], y_peer(1))
        total = total + ryrecv[w - 1].astype(F32)
    rxsend[...] = total.astype(BF16).reshape(4, 32, 512)
    for s in range(1, 4):
        send(rxsend.at[(x + s) % 4], rxrecv.at[s - 1], rx_send.at[s - 1], rx_recv.at[s - 1], x_peer(s))
    returned = rxsend[x].astype(F32)
    for s in range(1, 4):
        arrived(rxrecv.at[s - 1], rx_send.at[s - 1], rx_recv.at[s - 1], x_peer(s))
        returned = returned + rxrecv[s - 1].astype(F32)
    returned = returned.astype(BF16)
    row32 = iota((128, 32), 0)
    col32 = iota((128, 32), 1)
    placed = (row32 // 16 == col32 // 4) & (row32 % 8 == col32 % 4)
    first = (placed & ((row32 // 8) % 2 == 0)).astype(BF16)
    second = (placed & ((row32 // 8) % 2 == 1)).astype(BF16)
    homes = dot(first, returned[:, 0:256]) + dot(second, returned[:, 256:512])
    hsend[...] = homes.astype(BF16).reshape(8, 16, 256)
    for s in range(1, 8):
        send(hsend.at[(z + s) % 8], hrecv.at[z], h_send.at[s - 1], h_recv.at[s - 1], z_peer(s))
    hrecv[z] = hsend[z]
    for s in range(1, 8):
        arrived(hrecv.at[(z + 8 - s) % 8], h_send.at[s - 1], h_recv.at[s - 1], z_peer(s))

    projection = jnp.zeros((8, 1), F32)
    for n in range(16):
        cols = slice(n * 256, n * 256 + 256)
        piece = hrecv[n % 8].astype(F32)[(n // 8) * 8 : (n // 8) * 8 + 8]
        projection = projection + jnp.sum(piece * (state[:, cols] / root_mean), axis=1, keepdims=True)
    projection = projection / D
    sel_t = t_dot(sel_b, (iota((8, 128), 0) == iota((8, 128), 1)).astype(BF16))[:, 0:8].astype(BF16)
    kept = keep[...]

    def routed_backward(n, carry):
        cols = pl.ds(pl.multiple_of(n * 256, 256), 256)
        tile = hrecv[n % 8].astype(F32)
        piece = jnp.where(n < 8, tile[0:8], tile[8:16])
        normed = state[:, cols] / root_mean
        grad = (dlo[0:8, cols] + (piece - normed * projection) / root_mean) * occupied
        gx = spread(grad)
        p = prob[n]
        pb = p.astype(BF16)
        dp = dot_t(gx, v[:, cols])
        delta = jnp.sum(pb.astype(F32) * dp, axis=1, keepdims=True)
        sg = (p * (dp - delta)).astype(BF16)
        q_grad = (fold(dot(sg, k[:, cols])) * SCALE).astype(BF16)
        dq[:, cols] = dq[:, cols] + dot(sel_t, q_grad).astype(BF16)
        dko[:, cols] = (dkb[:, cols] + t_dot(sg, spread(qr[:, cols]))).astype(BF16)
        dvo[:, cols] = (dvb[:, cols] + t_dot(pb, gx)).astype(BF16)
        return carry

    lax.fori_loop(0, 16, routed_backward, 0, unroll=2)
    for n, (src, dst) in enumerate(((dq, dq_hbm), (dko, dk_hbm), (dvo, dv_hbm))):
        copy = pltpu.make_async_copy(src, dst, out_sem.at[2 + n])
        copy.start()
        outs.append(copy)
    for copy in outs:
        copy.wait()
    arrived(gu_hbm.at[:, other_cols], o_send.at[0], o_recv.at[0], pair_peer)
    arrived(gd_hbm.at[:, other_cols], o_send.at[1], o_recv.at[1], pair_peer)
    for copy in sent:
        copy.wait_send()


def local(query, key, value, resid, d_out, routes, gates, w_up, w_down):
    aux = jnp.concatenate([(routes == 0).astype(F32), gates], axis=1).T
    hbm = pl.BlockSpec(memory_space=pl.ANY)
    rows = (128, D)
    vm = pltpu.VMEM
    dma = pltpu.SemaphoreType.DMA
    return pl.pallas_call(
        kernel,
        out_shape=(
            jax.ShapeDtypeStruct(rows, BF16),
            jax.ShapeDtypeStruct(rows, BF16),
            jax.ShapeDtypeStruct(rows, BF16),
            jax.ShapeDtypeStruct((256, 1024), BF16),
            jax.ShapeDtypeStruct((256, 1024), BF16),
        ),
        in_specs=[pl.BlockSpec(memory_space=pltpu.VMEM)] + [hbm] * 7,
        out_specs=(hbm,) * 5,
        scratch_shapes=[
            vm(rows, BF16), vm(rows, BF16), vm(rows, BF16), vm(rows, BF16), vm(rows, BF16),
            vm((2, 256, 512), BF16), vm((2, 256, 512), BF16), vm((128, 128), BF16),
            vm((8, D), F32), vm((16, D), F32), vm((8, D), F32), vm((16, 32, 128), F32),
            vm((8, 16, 256), BF16), vm((8, 16, 256), BF16), vm((4, 2, 4, 4, 32, 256), BF16),
            vm((4, 8, 32, 1024), BF16), vm((4, 4, 32, 1024), BF16), vm((4, 4, 32, 1024), BF16),
            vm((4, 8, 32, 1024), BF16),
            vm((2, 256, 512), F32), vm((2, 256, 512), F32), vm((2, 256, 512), BF16), vm((2, 256, 512), BF16),
            vm((4, 2, 128, 512), BF16), vm((4, 128, 512), BF16), vm((4, 128, 512), BF16), vm((3, 128, 512), BF16),
            vm((4, 32, 512), BF16), vm((3, 32, 512), BF16), vm((8, 16, 256), BF16), vm((8, 16, 256), BF16),
            vm(rows, BF16), vm(rows, F32), vm(rows, F32), vm(rows, BF16), vm(rows, BF16),
            dma((7,)), dma((5,)), dma((2,)), dma((2,)), dma((7,)), dma((7,)), dma((3,)), dma((3,)),
            dma((4,)), dma((4,)), dma((3,)), dma((3,)),
            dma((4, 8)), dma((4, 8)), dma((4, 8)), dma((4, 8)), dma((4,)), dma((4,)), dma((3,)), dma((3,)),
            dma((3,)), dma((3,)), dma((7,)), dma((7,)), dma((2,)), dma((2,)),
        ],
        compiler_params=pltpu.CompilerParams(
            collective_id=0, has_side_effects=True, vmem_limit_bytes=48 * 1024 * 1024
        ),
    )(aux, query, key, value, resid, d_out, w_up, w_down)


def solution(mesh):
    tokens = P(("dp", "expert"), None)
    weights = P("dp", "expert")
    return jax.shard_map(
        local,
        mesh=mesh,
        in_specs=(tokens,) * 7 + (weights,) * 2,
        out_specs=(tokens,) * 3 + (weights,) * 2,
        check_vma=False,
    )
```

```python
import functools

import jax
import jax.numpy as jnp
from jax import lax
from jax.experimental import pallas as pl
from jax.experimental.pallas import tpu as pltpu
from jax.sharding import PartitionSpec as P

MESH = pl.DeviceIdType.MESH
F32 = jnp.float32
BF16 = jnp.bfloat16
D = 4096
SCALE = 0.125
EPS = 1e-06
Y_OFFSETS = (0, 1, 3, 2)
PAIRS = 32


def dot(a, b):
    return lax.dot_general(a, b, (((1,), (0,)), ((), ())), preferred_element_type=F32)


def dot_t(a, b):
    return lax.dot_general(a, b, (((1,), (1,)), ((), ())), preferred_element_type=F32)


def t_dot(a, b):
    return lax.dot_general(a, b, (((0,), (0,)), ((), ())), preferred_element_type=F32)


def iota(shape, dim):
    return lax.broadcasted_iota(jnp.int32, shape, dim)


def kernel(
    routes_ref, gates_ref, q_hbm, k_hbm, v_hbm, r_hbm, d_hbm, wu_hbm, wd_hbm,
    dq, dko, dvo, gu_hbm, gd_hbm,
    q, k, v, r, d, wu, wd, keep, qr, dlo, state, prob,
    asend, arecv, g, part, rs, ag, gu_acc, gd_acc, gu_out, gd_out,
    rsend, rcore, rysend, ryrecv, rxsend, rxrecv, hsend, hrecv,
    dkb, dvb,
    load_sem, out_sem, w_send, w_recv, a_send, a_recv, x_send, x_recv, c_send, c_recv, y_send, y_recv,
    rs_send, rs_recv, ag_send, ag_recv, rc_send, rc_recv, ry_send, ry_recv, rx_send, rx_recv, h_send, h_recv,
    o_send, o_recv,
):
    i = lax.axis_index("dp")
    j = lax.axis_index("expert")
    xl = i // 8
    z = i % 8
    y = j // 4
    xh = (j // 2) % 2
    c = j % 2
    x = xh * 2 + xl

    def dev(x_to, y_to, z_to, c_to):
        return ((x_to % 2) * 8 + z_to, y_to * 4 + (x_to // 2) * 2 + c_to)

    def z_peer(step):
        return dev(x, y, (z + step) % 8, c)

    def x_peer(step):
        return dev((x + step) % 4, y, z, c)

    def y_peer(step):
        return dev(x, (y + step) % 4, z, c)

    core_peer = dev(x, y, z, 1 - c)
    pair_peer = (((1 - xl) * 8 + z), j)

    barrier = pltpu.get_barrier_semaphore()
    peers = [z_peer(s) for s in range(1, 8)] + [x_peer(s) for s in range(1, 4)]
    peers += [y_peer(s) for s in range(1, 4)] + [core_peer]
    for peer in peers:
        pl.semaphore_signal(barrier, inc=1, device_id=peer, device_id_type=MESH)

    loads = []
    for n, (src, dst) in enumerate(((d_hbm, d), (q_hbm, q), (k_hbm, k), (r_hbm, r), (v_hbm, v))):
        loads.append(pltpu.make_async_copy(src, dst, load_sem.at[n]))
    own_cols = pl.ds(pl.multiple_of(xl * 512, 512), 512)
    other_cols = pl.ds(pl.multiple_of((1 - xl) * 512, 512), 512)
    loads.append(pltpu.make_async_copy(wd_hbm.at[:, own_cols], wd.at[xl], load_sem.at[5]))
    loads.append(pltpu.make_async_copy(wu_hbm.at[:, own_cols], wu.at[xl], load_sem.at[6]))
    for copy in loads:
        copy.start()

    sent = []

    def send(src, dst, send_sem, recv_sem, peer):
        copy = pltpu.make_async_remote_copy(
            src_ref=src, dst_ref=dst, send_sem=send_sem, recv_sem=recv_sem, device_id=peer, device_id_type=MESH
        )
        copy.start()
        sent.append(copy)

    def arrived(dst, send_sem, recv_sem, peer):
        pltpu.make_async_remote_copy(
            src_ref=dst, dst_ref=dst, send_sem=send_sem, recv_sem=recv_sem, device_id=peer, device_id_type=MESH
        ).wait_recv()

    flags = (routes_ref[...] == 0).astype(F32)
    picked = gates_ref[...] * flags
    gate_row = picked[0:1, :] + picked[1:2, :]
    hit = jnp.maximum(flags[0:1, :], flags[1:2, :])
    upper = (iota((128, 128), 0) <= iota((128, 128), 1)).astype(BF16)
    hits = jnp.broadcast_to(hit, (8, 128))
    rank = dot(hits.astype(BF16), upper) - 1.0
    slot = iota((8, 128), 0).astype(F32)
    sel = jnp.where((rank == slot) & (slot < 4.0), hits, 0.0)
    occupied = jnp.sum(sel, axis=1, keepdims=True)
    position = jnp.sum(sel * iota((8, 128), 1).astype(F32), axis=1, keepdims=True)
    gate = jnp.sum(sel * gate_row, axis=1, keepdims=True)
    sel_b = sel.astype(BF16)
    keep[...] = (1.0 - t_dot(sel_b, jnp.ones((8, 128), BF16))).astype(BF16)
    seen = iota((8, 128), 1).astype(F32) <= position
    seen32 = jnp.concatenate([seen] * 4, axis=0)
    lane_head = iota((8, 256), 1) // 64

    def spread(rows):
        return jnp.concatenate([jnp.where(lane_head == h, rows, 0.0) for h in range(4)], axis=0).astype(BF16)

    def fold(rows):
        total = jnp.where(lane_head == 0, rows[0:8], 0.0)
        for h in range(1, 4):
            total = total + jnp.where(lane_head == h, rows[8 * h : 8 * h + 8], 0.0)
        return total

    groups = [slice(n * 256, n * 256 + 256) for n in range(16)]
    loads[0].wait()
    for cols in groups:
        dlo[:, cols] = dot(sel_b, d[:, cols])
    for n in range(8):
        both = [gate * dlo[:, groups[n]], gate * dlo[:, groups[8 + n]]]
        asend[1, n] = jnp.concatenate(both, axis=0).astype(BF16)

    loads[1].wait()
    loads[2].wait()
    for cols in groups:
        qr[:, cols] = dot(sel_b, q[:, cols]) * SCALE
    scores = jnp.concatenate([dot_t(spread(qr[:, cols]), k[:, cols]) for cols in groups], axis=0)
    scores = jnp.where(jnp.concatenate([seen32] * 16, axis=0), scores, -jnp.inf)
    weights = jnp.exp(scores - jnp.max(scores, axis=1, keepdims=True))
    prob[...] = weights / jnp.sum(weights, axis=1, keepdims=True)

    pl.semaphore_wait(barrier, len(peers))

    def to_blocks(m):
        for s in range(1, 8):
            send(asend.at[m, (z + s) % 8], arecv.at[m, z], a_send.at[m, s - 1], a_recv.at[m, s - 1], z_peer(s))
        arecv[m, z] = asend[m, z]

    def send_weights(n):
        src, dst = ((wd_hbm, wd), (wu_hbm, wu))[n]
        for part_n in range(4):
            rows = slice(part_n * 64, part_n * 64 + 64)
            send(
                src.at[rows, other_cols], dst.at[xl, rows], w_send.at[n, part_n], w_recv.at[n, part_n], pair_peer
            )

    def weights_here(n):
        loads[5 + n].wait()
        dst = (wd, wu)[n]
        for part_n in range(4):
            rows = slice(part_n * 64, part_n * 64 + 64)
            arrived(dst.at[1 - xl, rows], w_send.at[n, part_n], w_recv.at[n, part_n], pair_peer)

    to_blocks(1)
    send_weights(0)

    loads[3].wait()
    loads[4].wait()
    for cols in groups:
        state[:, cols] = dot(sel_b, r[:, cols])
    squares = jnp.zeros((8, 256), F32)
    for n, cols in enumerate(groups):
        st = state[:, cols] + fold(dot(prob[n * 32 : n * 32 + 32, :].astype(BF16), v[:, cols]))
        state[:, cols] = st
        squares = squares + st * st
    squares = jnp.sum(squares, axis=1, keepdims=True)
    root_mean = jnp.sqrt(squares / D + EPS)
    for n in range(8):
        both = [state[:, groups[m]] / root_mean * occupied for m in (n, 8 + n)]
        asend[0, n] = jnp.concatenate(both, axis=0).astype(BF16)
    to_blocks(0)
    send_weights(1)

    lane0 = iota((128, 128), 1) < 64
    causal = iota((256, 128), 0) % 128 >= iota((256, 128), 1)

    def two(rows):
        zero = jnp.zeros_like(rows)
        return jnp.concatenate([jnp.where(lane0, rows, zero), jnp.where(lane0, zero, rows)], axis=0)

    def attend(n, carry):
        cols = pl.ds(pl.multiple_of(n * 128, 128), 128)
        k2 = k[:, cols]
        qs = two(q[:, cols] * jnp.asarray(SCALE, BF16))
        scores = jnp.where(causal, dot_t(qs, k2), -jnp.inf)
        weights = jnp.exp(scores - jnp.max(scores, axis=1, keepdims=True))
        p = weights / jnp.sum(weights, axis=1, keepdims=True)
        pb = p.astype(BF16)
        ds = two(d[:, cols] * keep[...])
        dp = dot_t(ds, v[:, cols])
        delta = jnp.sum(pb.astype(F32) * dp, axis=1, keepdims=True)
        sg = (p * (dp - delta)).astype(BF16)
        dkb[:, cols] = t_dot(sg, qs)
        dvb[:, cols] = t_dot(pb, ds)
        sides = jnp.concatenate([sg[:128], sg[128:]], axis=1)
        dq[:, cols] = (dot(sides, two(k2)) * SCALE).astype(BF16)
        return carry

    done_pairs = [0]

    def attend_some(count):
        first = done_pairs[0]
        last = min(PAIRS, first + count)
        if last > first:
            lax.fori_loop(first, last, attend, 0)
        done_pairs[0] = last

    row = iota((64, 128), 0)
    col = iota((64, 128), 1)
    permute = (row // 32 == (col // 8) % 2) & ((row % 32) // 4 == col // 16) & (row % 4 == col % 8)
    permute = permute.astype(BF16)

    def gather_x(m):
        for s in range(1, 8):
            arrived(arecv.at[m, (z + 8 - s) % 8], a_send.at[m, s - 1], a_recv.at[m, s - 1], z_peer(s))
        tiles = dot(permute, arecv[m].reshape(128, 256)).astype(BF16)
        block = g.at[m, y, c, x]
        block[...] = tiles.reshape(2, 32, 256)
        for s in range(1, 4):
            send(block, block, x_send.at[m, s - 1], x_recv.at[m, s - 1], x_peer(s))

    def gather_y(m):
        for s in range(1, 4):
            arrived(g.at[m, y, c, (x + 4 - s) % 4], x_send.at[m, s - 1], x_recv.at[m, s - 1], x_peer(s))
        block = g.at[m, y, c]
        send(block, block, c_send.at[m, 0], c_recv.at[m, 0], core_peer)
        send(block, block, y_send.at[m, 0], y_recv.at[m, 0], y_peer(3))
        send(block, block, y_send.at[m, 1], y_recv.at[m, 1], y_peer(1))

    def y_of(w):
        return (y + Y_OFFSETS[w]) % 4

    def rows_of(w, f, m):
        return g[m, y_of(w), :, :, f].reshape(256, 256)

    x_low = slice(0, 2)
    x_high = slice(2, 4)

    def gather(m, w):
        block = g.at[m, y_of(w), c]
        if w == 1:
            arrived(block, y_send.at[m, 0], y_recv.at[m, 0], y_peer(3))
            send(block.at[x_low], block.at[x_low], y_send.at[m, 2], y_recv.at[m, 2], y_peer(3))
        if w == 2:
            arrived(block, y_send.at[m, 1], y_recv.at[m, 1], y_peer(1))
            send(block.at[x_high], block.at[x_high], y_send.at[m, 3], y_recv.at[m, 3], y_peer(1))
        if w == 3:
            arrived(block.at[x_low], y_send.at[m, 2], y_recv.at[m, 2], y_peer(3))
            arrived(block.at[x_high], y_send.at[m, 3], y_recv.at[m, 3], y_peer(1))
        send(block, block, c_send.at[m, w], c_recv.at[m, w], core_peer)

    up_half = slice(0, 16)
    down_half = slice(16, 32)

    def reduce_start(m, w):
        arrived(g.at[m, y_of(w), 1 - c], c_send.at[m, w], c_recv.at[m, w], core_peer)
        right = (wu, wd)[m]
        terms = dot(rows_of(w, 0, m), right[0]) + dot(rows_of(w, 1, m), right[1])
        part[m, w] = terms.astype(BF16).reshape(8, 32, 512)
        far = part.at[m, w, (z + 4) % 8]
        ups, downs = rs.at[m, 0, w, 0], rs.at[m, 1, w, 0]
        send(far.at[up_half], ups.at[up_half], rs_send.at[m, 0, w, 0], rs_recv.at[m, 0, w, 0], z_peer(1))
        send(far.at[down_half], downs.at[down_half], rs_send.at[m, 1, w, 0], rs_recv.at[m, 1, w, 0], z_peer(7))

    def reduce_step(m, w, s):
        for side in range(2):
            block = (z + 4 - s) % 8 if side == 0 else (z + 4 + s) % 8
            here, fresh = (up_half, down_half) if side == 0 else (down_half, up_half)
            peer = z_peer(1) if side == 0 else z_peer(7)
            last = rs.at[m, side, w, s - 1]
            sems = rs_send.at[m, side, w, s - 1], rs_recv.at[m, side, w, s - 1]
            if s == 1:
                arrived(last.at[here], *sems, peer)
                last[here] = (last[here].astype(F32) + part[m, w, block, here].astype(F32)).astype(BF16)
                last[fresh] = part[m, w, block, fresh]
            else:
                arrived(last, *sems, peer)
                last[...] = (last[...].astype(F32) + part[m, w, block].astype(F32)).astype(BF16)
            send(last, rs.at[m, side, w, s], rs_send.at[m, side, w, s], rs_recv.at[m, side, w, s], peer)

    def reduced(m, w):
        total = part[m, w, z].astype(F32)
        for side in range(2):
            last = rs.at[m, side, w, 3]
            peer = z_peer(1) if side == 0 else z_peer(7)
            arrived(last, rs_send.at[m, side, w, 3], rs_recv.at[m, side, w, 3], peer)
            total = total + last[...].astype(F32)
        return total

    def activate(w):
        back = reduced(1, w)
        h = reduced(0, w)
        root = 0.7978845608028654
        inner = jnp.tanh(root * (h + 0.044715 * (h * h * h)))
        half = 0.5 * (1.0 + inner)
        slope = half + 0.5 * h * (1.0 - inner * inner) * (root * (1.0 + 3.0 * 0.044715 * (h * h)))
        ag[0, w, z] = (back * slope).astype(BF16)
        ag[1, w, z] = (h * half).astype(BF16)
        spread_out(0, w)

    def spread_out(m, w):
        send(ag.at[m, w, z], ag.at[m, w, z], ag_send.at[m, w, 0], ag_recv.at[m, w, 0], z_peer(1))
        send(ag.at[m, w, z], ag.at[m, w, z], ag_send.at[m, w, 4], ag_recv.at[m, w, 4], z_peer(7))

    def forward(m, w, s):
        up = (z + 8 - s) % 8
        down = (z + s) % 8
        block = ag.at[m, w, up]
        arrived(block, ag_send.at[m, w, s - 1], ag_recv.at[m, w, s - 1], z_peer(1))
        block = block.at[up_half] if s == 3 else block
        send(block, block, ag_send.at[m, w, s], ag_recv.at[m, w, s], z_peer(1))
        block = ag.at[m, w, down]
        arrived(block, ag_send.at[m, w, 3 + s], ag_recv.at[m, w, 3 + s], z_peer(7))
        block = block.at[down_half] if s == 3 else block
        send(block, block, ag_send.at[m, w, 4 + s], ag_recv.at[m, w, 4 + s], z_peer(7))

    def whole(m, w):
        far = (z + 4) % 8
        arrived(ag.at[m, w, far, up_half], ag_send.at[m, w, 3], ag_recv.at[m, w, 3], z_peer(1))
        arrived(ag.at[m, w, far, down_half], ag_send.at[m, w, 7], ag_recv.at[m, w, 7], z_peer(7))

    def input_gradient(w):
        whole(0, w)
        hidden_grad = ag[0, w].reshape(256, 512)
        for f in range(2):
            back = dot_t(hidden_grad, wu[f]).astype(BF16)
            rsend[w, :, :, f * 256 : f * 256 + 256] = back.reshape(2, 128, 256)
        send(rsend.at[w, 1 - c], rcore.at[w], rc_send.at[w], rc_recv.at[w], core_peer)

    def weight_gradient(m, w):
        acc, out = ((gu_acc, gu_out), (gd_acc, gd_out))[m]
        right = ag[m, w].reshape(256, 512)
        for f in range(2):
            term = t_dot(rows_of(w, f, m), right)
            if w == 0:
                acc[f] = term
            elif w < 3:
                acc[f] += term
            else:
                out[f] = (acc[f] + term).astype(BF16)

    def give_back(w):
        arrived(rcore.at[w], rc_send.at[w], rc_recv.at[w], core_peer)
        total = rsend[w, c].astype(F32) + rcore[w].astype(F32)
        rysend[w] = total.astype(BF16)
        if w > 0:
            send(rysend.at[w], ryrecv.at[w - 1], ry_send.at[w - 1], ry_recv.at[w - 1], y_peer(Y_OFFSETS[w]))

    def sum_y():
        total = rysend[0].astype(F32)
        for w in range(1, 4):
            arrived(ryrecv.at[w - 1], ry_send.at[w - 1], ry_recv.at[w - 1], y_peer(1))
            total = total + ryrecv[w - 1].astype(F32)
        rxsend[...] = total.astype(BF16).reshape(4, 32, 512)
        for s in range(1, 4):
            send(rxsend.at[(x + s) % 4], rxrecv.at[s - 1], rx_send.at[s - 1], rx_recv.at[s - 1], x_peer(s))

    def sum_x():
        returned = rxsend[x].astype(F32)
        for s in range(1, 4):
            arrived(rxrecv.at[s - 1], rx_send.at[s - 1], rx_recv.at[s - 1], x_peer(s))
            returned = returned + rxrecv[s - 1].astype(F32)
        returned = returned.astype(BF16)
        row32 = iota((128, 32), 0)
        col32 = iota((128, 32), 1)
        placed = (row32 // 16 == col32 // 4) & (row32 % 8 == col32 % 4)
        first = (placed & ((row32 // 8) % 2 == 0)).astype(BF16)
        second = (placed & ((row32 // 8) % 2 == 1)).astype(BF16)
        homes = dot(first, returned[:, 0:256]) + dot(second, returned[:, 256:512])
        hsend[...] = homes.astype(BF16).reshape(8, 16, 256)
        for s in range(1, 8):
            send(hsend.at[(z + s) % 8], hrecv.at[z], h_send.at[s - 1], h_recv.at[s - 1], z_peer(s))
        hrecv[z] = hsend[z]

    outs = []

    def hand_over(m):
        out, whole_out = ((gu_out, gu_hbm), (gd_out, gd_hbm))[m]
        send(out.at[1 - xl], whole_out.at[:, own_cols], o_send.at[m], o_recv.at[m], pair_peer)
        copy = pltpu.make_async_copy(out.at[xl], whole_out.at[:, own_cols], out_sem.at[m])
        copy.start()
        outs.append(copy)

    plan = [
        (attend_some, 2), (gather_x, 1), (attend_some, 7), (gather_y, 1), (gather_x, 0), (attend_some, 1),
        (weights_here, 0), (reduce_start, 1, 0), (attend_some, 4), (gather_y, 0), (reduce_step, 1, 0, 1),
        (gather, 1, 2), (gather, 1, 1), (weights_here, 1), (reduce_start, 0, 0), (reduce_start, 1, 2),
        (reduce_start, 1, 1), (reduce_step, 1, 0, 2), (attend_some, 1), (reduce_step, 0, 0, 1), (gather, 0, 2),
        (gather, 0, 1), (reduce_step, 1, 2, 1), (attend_some, 1), (reduce_step, 1, 1, 1), (gather, 1, 3),
        (reduce_start, 0, 1), (reduce_step, 1, 0, 3), (reduce_start, 1, 3), (reduce_step, 0, 0, 2),
        (gather, 0, 3), (reduce_step, 1, 2, 2), (reduce_start, 0, 2), (reduce_step, 1, 1, 2),
        (reduce_step, 0, 1, 1), (reduce_start, 0, 3), (reduce_step, 1, 3, 1), (reduce_step, 0, 0, 3),
        (attend_some, 1), (reduce_step, 1, 2, 3), (reduce_step, 0, 2, 1), (attend_some, 1),
        (reduce_step, 1, 1, 3), (attend_some, 1), (reduce_step, 0, 1, 2), (reduce_step, 0, 3, 1),
        (attend_some, 1), (reduce_step, 1, 3, 2), (attend_some, 1), (activate, 0), (attend_some, 2),
        (reduce_step, 0, 2, 2), (attend_some, 2), (reduce_step, 0, 1, 3), (attend_some, 1),
        (reduce_step, 0, 3, 2), (attend_some, 1), (reduce_step, 1, 3, 3), (attend_some, 1), (forward, 0, 0, 1),
        (attend_some, 1), (reduce_step, 0, 2, 3), (attend_some, 1), (activate, 1), (reduce_step, 0, 3, 3),
        (attend_some, 2), (forward, 0, 0, 2), (activate, 2), (forward, 0, 1, 1), (activate, 3),
        (forward, 0, 0, 3), (forward, 0, 2, 1), (forward, 0, 1, 2), (forward, 0, 3, 1), (input_gradient, 0),
        (weight_gradient, 0, 0), (give_back, 0), (forward, 0, 1, 3), (forward, 0, 2, 2), (forward, 0, 3, 2),
        (input_gradient, 1), (forward, 0, 2, 3), (weight_gradient, 0, 1), (give_back, 1), (forward, 0, 3, 3),
        (spread_out, 1, 0), (spread_out, 1, 1), (spread_out, 1, 2), (spread_out, 1, 3), (input_gradient, 2),
        (weight_gradient, 0, 2), (give_back, 2), (input_gradient, 3), (forward, 1, 0, 1), (forward, 1, 1, 1),
        (weight_gradient, 0, 3), (give_back, 3), (forward, 1, 2, 1), (forward, 1, 3, 1), (forward, 1, 0, 2),
        (forward, 1, 1, 2), (forward, 1, 2, 2), (forward, 1, 3, 2), (forward, 1, 0, 3), (sum_y,), (hand_over, 0),
        (forward, 1, 1, 3), (forward, 1, 2, 3), (forward, 1, 3, 3), (whole, 1, 0), (weight_gradient, 1, 0),
        (whole, 1, 1), (weight_gradient, 1, 1), (sum_x,), (whole, 1, 2), (weight_gradient, 1, 2), (whole, 1, 3),
        (weight_gradient, 1, 3), (hand_over, 1),
    ]
    for step, *which in plan:
        step(*which)
    attend_some(PAIRS)
    for s in range(1, 8):
        arrived(hrecv.at[(z + 8 - s) % 8], h_send.at[s - 1], h_recv.at[s - 1], z_peer(s))

    def piece(n):
        return hrecv[n % 8].astype(F32)[(n // 8) * 8 : (n // 8) * 8 + 8]

    inverse = 1.0 / root_mean
    projection = jnp.zeros((8, 256), F32)
    for n, cols in enumerate(groups):
        projection = projection + piece(n) * (state[:, cols] * inverse)
    projection = jnp.sum(projection, axis=1, keepdims=True) / D
    sel_t = t_dot(sel_b, (iota((8, 128), 0) == iota((8, 128), 1)).astype(BF16))[:, 0:8].astype(BF16)
    spreads = []
    for n, cols in enumerate(groups):
        normed = state[:, cols] * inverse
        grad = (dlo[:, cols] + (piece(n) - normed * projection) * inverse) * occupied
        spreads.append(spread(grad))
    p = prob[...]
    pb = p.astype(BF16)
    dp = jnp.concatenate([dot_t(spreads[n], v[:, cols]) for n, cols in enumerate(groups)], axis=0)
    delta = jnp.sum(pb.astype(F32) * dp, axis=1, keepdims=True)
    sg = (p * (dp - delta)).astype(BF16)
    for n, cols in enumerate(groups):
        mine = slice(n * 32, n * 32 + 32)
        q_grad = (fold(dot(sg[mine], k[:, cols])) * SCALE).astype(BF16)
        dq[:, cols] = dq[:, cols] + dot(sel_t, q_grad).astype(BF16)
        dko[:, cols] = (dkb[:, cols] + t_dot(sg[mine], spread(qr[:, cols]))).astype(BF16)
        dvo[:, cols] = (dvb[:, cols] + t_dot(pb[mine], spreads[n])).astype(BF16)

    for copy in outs:
        copy.wait()
    arrived(gu_hbm.at[:, other_cols], o_send.at[0], o_recv.at[0], pair_peer)
    arrived(gd_hbm.at[:, other_cols], o_send.at[1], o_recv.at[1], pair_peer)
    for copy in sent:
        copy.wait_send()


def write_out(*refs):
    sems = refs[10]
    copies = [pltpu.make_async_copy(refs[n], refs[5 + n], sems.at[n]) for n in range(5)]
    for copy in copies:
        copy.start()
    for copy in copies:
        copy.wait()


def local(query, key, value, resid, d_out, routes, gates, w_up, w_down):
    hbm = pl.BlockSpec(memory_space=pl.ANY)
    pinned = pl.BlockSpec(memory_space=pltpu.HBM)
    vmem = pl.BlockSpec(memory_space=pltpu.VMEM)
    rows = (128, D)
    vm = pltpu.VMEM
    dma = pltpu.SemaphoreType.DMA
    results = pl.pallas_call(
        kernel,
        out_shape=(
            jax.ShapeDtypeStruct(rows, BF16),
            jax.ShapeDtypeStruct(rows, BF16),
            jax.ShapeDtypeStruct(rows, BF16),
            jax.ShapeDtypeStruct((256, 1024), BF16),
            jax.ShapeDtypeStruct((256, 1024), BF16),
        ),
        in_specs=[vmem, vmem] + [hbm] * 5 + [pinned] * 2,
        out_specs=(vmem,) * 3 + (hbm,) * 2,
        scratch_shapes=[
            vm(rows, BF16), vm(rows, BF16), vm(rows, BF16), vm(rows, BF16), vm(rows, BF16),
            vm((2, 256, 512), BF16), vm((2, 256, 512), BF16), vm((128, 128), BF16),
            vm((8, D), F32), vm((8, D), F32), vm((8, D), F32), vm((512, 128), F32),
            vm((2, 8, 16, 256), BF16), vm((2, 8, 16, 256), BF16), vm((2, 4, 2, 4, 2, 32, 256), BF16),
            vm((2, 4, 8, 32, 512), BF16), vm((2, 2, 4, 4, 32, 512), BF16),
            vm((2, 4, 8, 32, 512), BF16),
            vm((2, 256, 512), F32), vm((2, 256, 512), F32), vm((2, 256, 512), BF16), vm((2, 256, 512), BF16),
            vm((4, 2, 128, 512), BF16), vm((4, 128, 512), BF16), vm((4, 128, 512), BF16), vm((3, 128, 512), BF16),
            vm((4, 32, 512), BF16), vm((3, 32, 512), BF16), vm((8, 16, 256), BF16), vm((8, 16, 256), BF16),
            vm(rows, F32), vm(rows, F32),
            dma((7,)), dma((2,)), dma((2, 4)), dma((2, 4)), dma((2, 7)), dma((2, 7)), dma((2, 3)), dma((2, 3)),
            dma((2, 4)), dma((2, 4)), dma((2, 4)), dma((2, 4)),
            dma((2, 2, 4, 4)), dma((2, 2, 4, 4)), dma((2, 4, 8)), dma((2, 4, 8)), dma((4,)), dma((4,)), dma((3,)), dma((3,)),
            dma((3,)), dma((3,)), dma((7,)), dma((7,)), dma((2,)), dma((2,)),
        ],
        compiler_params=pltpu.CompilerParams(
            collective_id=0, has_side_effects=True, vmem_limit_bytes=61180000
        ),
    )(routes.T, gates.T, query, key, value, resid, d_out, w_up, w_down)
    return pl.pallas_call(
        write_out,
        out_shape=tuple(jax.ShapeDtypeStruct(part.shape, part.dtype) for part in results),
        in_specs=[vmem] * 5,
        out_specs=(hbm,) * 5,
        scratch_shapes=[dma((5,))],
    )(*results)


def solution(mesh):
    tokens = P(("dp", "expert"), None)
    weights = P("dp", "expert")
    return jax.shard_map(
        local,
        mesh=mesh,
        in_specs=(tokens,) * 7 + (weights,) * 2,
        out_specs=(tokens,) * 3 + (weights,) * 2,
        check_vma=False,
    )
```

```python
import functools

import jax
import jax.numpy as jnp
from jax import lax
from jax.experimental import pallas as pl
from jax.experimental.pallas import tpu as pltpu
from jax.sharding import PartitionSpec as P

MESH = pl.DeviceIdType.MESH
F32 = jnp.float32
BF16 = jnp.bfloat16
D = 4096
SCALE = 0.125
EPS = 1e-06
Y_OFFSETS = (0, 1, 3, 2)
PAIRS = 32


def dot(a, b):
    return lax.dot_general(a, b, (((1,), (0,)), ((), ())), preferred_element_type=F32)


def dot_t(a, b):
    return lax.dot_general(a, b, (((1,), (1,)), ((), ())), preferred_element_type=F32)


def t_dot(a, b):
    return lax.dot_general(a, b, (((0,), (0,)), ((), ())), preferred_element_type=F32)


def iota(shape, dim):
    return lax.broadcasted_iota(jnp.int32, shape, dim)


def kernel(
    routes_ref, gates_ref, q_hbm, k_hbm, v_hbm, r_hbm, d_hbm, wu_hbm, wd_hbm,
    dq, dko, dvo, gu_hbm, gd_hbm,
    q, k, v, r, d, wu, wd, wx, keep, qr, dlo, state, prob,
    asend, arecv, g, part, rs, ag, gu_acc, gd_acc, gu_out, gd_out,
    rsend, rcore, rysend, ryrecv, rxsend, rxrecv, hsend, hrecv,
    dkb, dvb,
    load_sem, out_sem, w_send, w_recv, a_send, a_recv, x_send, x_recv, c_send, c_recv, y_send, y_recv,
    rs_send, rs_recv, ag_send, ag_recv, rc_send, rc_recv, ry_send, ry_recv, rx_send, rx_recv, h_send, h_recv,
    o_send, o_recv,
):
    i = lax.axis_index("dp")
    j = lax.axis_index("expert")
    xl = i // 8
    z = i % 8
    y = j // 4
    xh = (j // 2) % 2
    c = j % 2
    x = xh * 2 + xl

    def dev(x_to, y_to, z_to, c_to):
        return ((x_to % 2) * 8 + z_to, y_to * 4 + (x_to // 2) * 2 + c_to)

    def z_peer(step):
        return dev(x, y, (z + step) % 8, c)

    def x_peer(step):
        return dev((x + step) % 4, y, z, c)

    def y_peer(step):
        return dev(x, (y + step) % 4, z, c)

    core_peer = dev(x, y, z, 1 - c)
    pair_peer = (((1 - xl) * 8 + z), j)

    barrier = pltpu.get_barrier_semaphore()
    peers = [z_peer(s) for s in range(1, 8)] + [x_peer(s) for s in range(1, 4)]
    peers += [y_peer(s) for s in range(1, 4)] + [core_peer]
    for peer in peers:
        pl.semaphore_signal(barrier, inc=1, device_id=peer, device_id_type=MESH)

    loads = []
    for n, (src, dst) in enumerate(((d_hbm, d), (q_hbm, q), (k_hbm, k), (r_hbm, r), (v_hbm, v))):
        loads.append(pltpu.make_async_copy(src, dst, load_sem.at[n]))
    own_cols = pl.ds(pl.multiple_of(xl * 512, 512), 512)
    other_cols = pl.ds(pl.multiple_of((1 - xl) * 512, 512), 512)
    loads.append(pltpu.make_async_copy(wd_hbm.at[:, own_cols], wd.at[xl], load_sem.at[5]))
    loads.append(pltpu.make_async_copy(wu_hbm.at[:, own_cols], wu.at[xl], load_sem.at[6]))
    loads.append(pltpu.make_async_copy(wd_hbm.at[:, other_cols], wx.at[0], load_sem.at[7]))
    loads.append(pltpu.make_async_copy(wu_hbm.at[:, other_cols], wx.at[1], load_sem.at[8]))
    for copy in loads:
        copy.start()

    sent = []

    def send(src, dst, send_sem, recv_sem, peer):
        copy = pltpu.make_async_remote_copy(
            src_ref=src, dst_ref=dst, send_sem=send_sem, recv_sem=recv_sem, device_id=peer, device_id_type=MESH
        )
        copy.start()
        sent.append(copy)

    def arrived(dst, send_sem, recv_sem, peer):
        pltpu.make_async_remote_copy(
            src_ref=dst, dst_ref=dst, send_sem=send_sem, recv_sem=recv_sem, device_id=peer, device_id_type=MESH
        ).wait_recv()

    flags = (routes_ref[...] == 0).astype(F32)
    picked = gates_ref[...] * flags
    gate_row = picked[0:1, :] + picked[1:2, :]
    hit = jnp.maximum(flags[0:1, :], flags[1:2, :])
    upper = (iota((128, 128), 0) <= iota((128, 128), 1)).astype(BF16)
    hits = jnp.broadcast_to(hit, (8, 128))
    rank = dot(hits.astype(BF16), upper) - 1.0
    slot = iota((8, 128), 0).astype(F32)
    sel = jnp.where((rank == slot) & (slot < 4.0), hits, 0.0)
    occupied = jnp.sum(sel, axis=1, keepdims=True)
    position = jnp.sum(sel * iota((8, 128), 1).astype(F32), axis=1, keepdims=True)
    gate = jnp.sum(sel * gate_row, axis=1, keepdims=True)
    sel_b = sel.astype(BF16)
    keep[...] = (1.0 - t_dot(sel_b, jnp.ones((8, 128), BF16))).astype(BF16)
    seen = iota((8, 128), 1).astype(F32) <= position
    seen32 = jnp.concatenate([seen] * 4, axis=0)
    lane_head = iota((8, 256), 1) // 64

    def spread(rows):
        return jnp.concatenate([jnp.where(lane_head == h, rows, 0.0) for h in range(4)], axis=0).astype(BF16)

    def fold(rows):
        total = jnp.where(lane_head == 0, rows[0:8], 0.0)
        for h in range(1, 4):
            total = total + jnp.where(lane_head == h, rows[8 * h : 8 * h + 8], 0.0)
        return total

    groups = [slice(n * 256, n * 256 + 256) for n in range(16)]
    loads[0].wait()
    for cols in groups:
        dlo[:, cols] = dot(sel_b, d[:, cols])
    for n in range(8):
        both = [gate * dlo[:, groups[n]], gate * dlo[:, groups[8 + n]]]
        asend[1, n] = jnp.concatenate(both, axis=0).astype(BF16)

    loads[1].wait()
    loads[2].wait()
    for cols in groups:
        qr[:, cols] = dot(sel_b, q[:, cols]) * SCALE
    scores = jnp.concatenate([dot_t(spread(qr[:, cols]), k[:, cols]) for cols in groups], axis=0)
    scores = jnp.where(jnp.concatenate([seen32] * 16, axis=0), scores, -jnp.inf)
    weights = jnp.exp(scores - jnp.max(scores, axis=1, keepdims=True))
    prob[...] = weights / jnp.sum(weights, axis=1, keepdims=True)

    pl.semaphore_wait(barrier, len(peers))

    def to_blocks(m):
        for s in range(1, 8):
            send(asend.at[m, (z + s) % 8], arecv.at[m, z], a_send.at[m, s - 1], a_recv.at[m, s - 1], z_peer(s))
        arecv[m, z] = asend[m, z]

    def send_weights(n):
        dst = (wd, wu)[n]
        loads[7 + n].wait()
        for part_n in range(4):
            rows = slice(part_n * 64, part_n * 64 + 64)
            send(
                wx.at[n, rows], dst.at[xl, rows], w_send.at[n, part_n], w_recv.at[n, part_n], pair_peer
            )

    def weights_here(n):
        loads[5 + n].wait()
        dst = (wd, wu)[n]
        for part_n in range(4):
            rows = slice(part_n * 64, part_n * 64 + 64)
            arrived(dst.at[1 - xl, rows], w_send.at[n, part_n], w_recv.at[n, part_n], pair_peer)

    send_weights(0)
    to_blocks(1)

    loads[3].wait()
    loads[4].wait()
    for cols in groups:
        state[:, cols] = dot(sel_b, r[:, cols])
    squares = jnp.zeros((8, 256), F32)
    for n, cols in enumerate(groups):
        st = state[:, cols] + fold(dot(prob[n * 32 : n * 32 + 32, :].astype(BF16), v[:, cols]))
        state[:, cols] = st
        squares = squares + st * st
    squares = jnp.sum(squares, axis=1, keepdims=True)
    root_mean = jnp.sqrt(squares / D + EPS)
    for n in range(8):
        both = [state[:, groups[m]] / root_mean * occupied for m in (n, 8 + n)]
        asend[0, n] = jnp.concatenate(both, axis=0).astype(BF16)
    to_blocks(0)

    lane0 = iota((128, 128), 1) < 64
    causal = iota((256, 128), 0) % 128 >= iota((256, 128), 1)

    def two(rows):
        zero = jnp.zeros_like(rows)
        return jnp.concatenate([jnp.where(lane0, rows, zero), jnp.where(lane0, zero, rows)], axis=0)

    def attend(n, carry):
        cols = pl.ds(pl.multiple_of(n * 128, 128), 128)
        k2 = k[:, cols]
        qs = two(q[:, cols] * jnp.asarray(SCALE, BF16))
        scores = jnp.where(causal, dot_t(qs, k2), -jnp.inf)
        weights = jnp.exp(scores - jnp.max(scores, axis=1, keepdims=True))
        p = weights / jnp.sum(weights, axis=1, keepdims=True)
        pb = p.astype(BF16)
        ds = two(d[:, cols] * keep[...])
        dp = dot_t(ds, v[:, cols])
        delta = jnp.sum(pb.astype(F32) * dp, axis=1, keepdims=True)
        sg = (p * (dp - delta)).astype(BF16)
        dkb[:, cols] = t_dot(sg, qs)
        dvb[:, cols] = t_dot(pb, ds)
        sides = jnp.concatenate([sg[:128], sg[128:]], axis=1)
        dq[:, cols] = (dot(sides, two(k2)) * SCALE).astype(BF16)
        return carry

    done_pairs = [0]

    def attend_some(count):
        first = done_pairs[0]
        last = min(PAIRS, first + count)
        if last > first:
            lax.fori_loop(first, last, attend, 0)
        done_pairs[0] = last

    row = iota((64, 128), 0)
    col = iota((64, 128), 1)
    permute = (row // 32 == (col // 8) % 2) & ((row % 32) // 4 == col // 16) & (row % 4 == col % 8)
    permute = permute.astype(BF16)

    def gather_x(m):
        for s in range(1, 8):
            arrived(arecv.at[m, (z + 8 - s) % 8], a_send.at[m, s - 1], a_recv.at[m, s - 1], z_peer(s))
        tiles = dot(permute, arecv[m].reshape(128, 256)).astype(BF16)
        block = g.at[m, y, c, x]
        block[...] = tiles.reshape(2, 32, 256)
        for s in range(1, 4):
            send(block, block, x_send.at[m, s - 1], x_recv.at[m, s - 1], x_peer(s))

    def gather_y(m):
        for s in range(1, 4):
            arrived(g.at[m, y, c, (x + 4 - s) % 4], x_send.at[m, s - 1], x_recv.at[m, s - 1], x_peer(s))
        block = g.at[m, y, c]
        send(block, block, c_send.at[m, 0], c_recv.at[m, 0], core_peer)
        send(block, block, y_send.at[m, 0], y_recv.at[m, 0], y_peer(3))
        send(block, block, y_send.at[m, 1], y_recv.at[m, 1], y_peer(1))

    def y_of(w):
        return (y + Y_OFFSETS[w]) % 4

    def rows_of(w, f, m):
        return g[m, y_of(w), :, :, f].reshape(256, 256)

    x_low = slice(0, 2)
    x_high = slice(2, 4)

    def gather(m, w):
        block = g.at[m, y_of(w), c]
        if w == 1:
            arrived(block, y_send.at[m, 0], y_recv.at[m, 0], y_peer(3))
            send(block.at[x_low], block.at[x_low], y_send.at[m, 2], y_recv.at[m, 2], y_peer(3))
        if w == 2:
            arrived(block, y_send.at[m, 1], y_recv.at[m, 1], y_peer(1))
            send(block.at[x_high], block.at[x_high], y_send.at[m, 3], y_recv.at[m, 3], y_peer(1))
        if w == 3:
            arrived(block.at[x_low], y_send.at[m, 2], y_recv.at[m, 2], y_peer(3))
            arrived(block.at[x_high], y_send.at[m, 3], y_recv.at[m, 3], y_peer(1))
        send(block, block, c_send.at[m, w], c_recv.at[m, w], core_peer)

    up_half = slice(0, 16)
    down_half = slice(16, 32)

    def reduce_start(m, w):
        arrived(g.at[m, y_of(w), 1 - c], c_send.at[m, w], c_recv.at[m, w], core_peer)
        right = (wu, wd)[m]
        terms = dot(rows_of(w, 0, m), right[0]) + dot(rows_of(w, 1, m), right[1])
        part[m, w] = terms.astype(BF16).reshape(8, 32, 512)
        far = part.at[m, w, (z + 4) % 8]
        ups, downs = rs.at[m, 0, w, 0], rs.at[m, 1, w, 0]
        send(far.at[up_half], ups.at[up_half], rs_send.at[m, 0, w, 0], rs_recv.at[m, 0, w, 0], z_peer(1))
        send(far.at[down_half], downs.at[down_half], rs_send.at[m, 1, w, 0], rs_recv.at[m, 1, w, 0], z_peer(7))

    def reduce_step(m, w, s):
        for side in range(2):
            block = (z + 4 - s) % 8 if side == 0 else (z + 4 + s) % 8
            here, fresh = (up_half, down_half) if side == 0 else (down_half, up_half)
            peer = z_peer(1) if side == 0 else z_peer(7)
            last = rs.at[m, side, w, s - 1]
            sems = rs_send.at[m, side, w, s - 1], rs_recv.at[m, side, w, s - 1]
            if s == 1:
                arrived(last.at[here], *sems, peer)
                last[here] = (last[here].astype(F32) + part[m, w, block, here].astype(F32)).astype(BF16)
                last[fresh] = part[m, w, block, fresh]
            else:
                arrived(last, *sems, peer)
                last[...] = (last[...].astype(F32) + part[m, w, block].astype(F32)).astype(BF16)
            send(last, rs.at[m, side, w, s], rs_send.at[m, side, w, s], rs_recv.at[m, side, w, s], peer)

    def reduced(m, w):
        total = part[m, w, z].astype(F32)
        for side in range(2):
            last = rs.at[m, side, w, 3]
            peer = z_peer(1) if side == 0 else z_peer(7)
            arrived(last, rs_send.at[m, side, w, 3], rs_recv.at[m, side, w, 3], peer)
            total = total + last[...].astype(F32)
        return total

    def activate(w):
        back = reduced(1, w)
        h = reduced(0, w)
        root = 0.7978845608028654
        inner = jnp.tanh(root * (h + 0.044715 * (h * h * h)))
        half = 0.5 * (1.0 + inner)
        slope = half + 0.5 * h * (1.0 - inner * inner) * (root * (1.0 + 3.0 * 0.044715 * (h * h)))
        ag[0, w, z] = (back * slope).astype(BF16)
        ag[1, w, z] = (h * half).astype(BF16)
        spread_out(0, w)

    def spread_out(m, w):
        send(ag.at[m, w, z], ag.at[m, w, z], ag_send.at[m, w, 0], ag_recv.at[m, w, 0], z_peer(1))
        send(ag.at[m, w, z], ag.at[m, w, z], ag_send.at[m, w, 4], ag_recv.at[m, w, 4], z_peer(7))

    def forward(m, w, s):
        up = (z + 8 - s) % 8
        down = (z + s) % 8
        block = ag.at[m, w, up]
        arrived(block, ag_send.at[m, w, s - 1], ag_recv.at[m, w, s - 1], z_peer(1))
        block = block.at[up_half] if s == 3 else block
        send(block, block, ag_send.at[m, w, s], ag_recv.at[m, w, s], z_peer(1))
        block = ag.at[m, w, down]
        arrived(block, ag_send.at[m, w, 3 + s], ag_recv.at[m, w, 3 + s], z_peer(7))
        block = block.at[down_half] if s == 3 else block
        send(block, block, ag_send.at[m, w, 4 + s], ag_recv.at[m, w, 4 + s], z_peer(7))

    def whole(m, w):
        far = (z + 4) % 8
        arrived(ag.at[m, w, far, up_half], ag_send.at[m, w, 3], ag_recv.at[m, w, 3], z_peer(1))
        arrived(ag.at[m, w, far, down_half], ag_send.at[m, w, 7], ag_recv.at[m, w, 7], z_peer(7))

    def input_gradient(w):
        whole(0, w)
        hidden_grad = ag[0, w].reshape(256, 512)
        for f in range(2):
            back = dot_t(hidden_grad, wu[f]).astype(BF16)
            rsend[w, :, :, f * 256 : f * 256 + 256] = back.reshape(2, 128, 256)
        send(rsend.at[w, 1 - c], rcore.at[w], rc_send.at[w], rc_recv.at[w], core_peer)

    def weight_gradient(m, w):
        acc, out = ((gu_acc, gu_out), (gd_acc, gd_out))[m]
        right = ag[m, w].reshape(256, 512)
        for f in range(2):
            term = t_dot(rows_of(w, f, m), right)
            if w == 0:
                acc[f] = term
            elif w < 3:
                acc[f] += term
            else:
                out[f] = (acc[f] + term).astype(BF16)

    def give_back(w):
        arrived(rcore.at[w], rc_send.at[w], rc_recv.at[w], core_peer)
        total = rsend[w, c].astype(F32) + rcore[w].astype(F32)
        rysend[w] = total.astype(BF16)
        if w > 0:
            send(rysend.at[w], ryrecv.at[w - 1], ry_send.at[w - 1], ry_recv.at[w - 1], y_peer(Y_OFFSETS[w]))

    def sum_y():
        total = rysend[0].astype(F32)
        for w in range(1, 4):
            arrived(ryrecv.at[w - 1], ry_send.at[w - 1], ry_recv.at[w - 1], y_peer(1))
            total = total + ryrecv[w - 1].astype(F32)
        rxsend[...] = total.astype(BF16).reshape(4, 32, 512)
        for s in range(1, 4):
            send(rxsend.at[(x + s) % 4], rxrecv.at[s - 1], rx_send.at[s - 1], rx_recv.at[s - 1], x_peer(s))

    def sum_x():
        returned = rxsend[x].astype(F32)
        for s in range(1, 4):
            arrived(rxrecv.at[s - 1], rx_send.at[s - 1], rx_recv.at[s - 1], x_peer(s))
            returned = returned + rxrecv[s - 1].astype(F32)
        returned = returned.astype(BF16)
        row32 = iota((128, 32), 0)
        col32 = iota((128, 32), 1)
        placed = (row32 // 16 == col32 // 4) & (row32 % 8 == col32 % 4)
        first = (placed & ((row32 // 8) % 2 == 0)).astype(BF16)
        second = (placed & ((row32 // 8) % 2 == 1)).astype(BF16)
        homes = dot(first, returned[:, 0:256]) + dot(second, returned[:, 256:512])
        hsend[...] = homes.astype(BF16).reshape(8, 16, 256)
        for s in range(1, 8):
            send(hsend.at[(z + s) % 8], hrecv.at[z], h_send.at[s - 1], h_recv.at[s - 1], z_peer(s))
        hrecv[z] = hsend[z]

    outs = []

    def hand_over(m):
        out, whole_out = ((gu_out, gu_hbm), (gd_out, gd_hbm))[m]
        send(out.at[1 - xl], whole_out.at[:, own_cols], o_send.at[m], o_recv.at[m], pair_peer)
        copy = pltpu.make_async_copy(out.at[xl], whole_out.at[:, own_cols], out_sem.at[m])
        copy.start()
        outs.append(copy)

    plan = [
        (attend_some, 2), (gather_x, 1), (attend_some, 4), (gather_x, 0), (send_weights, 1), (gather_y, 1),
        (attend_some, 1), (weights_here, 0), (reduce_start, 1, 0), (attend_some, 2), (gather_y, 0),
        (gather, 1, 1), (gather, 1, 2), (reduce_start, 1, 1), (reduce_start, 1, 2), (weights_here, 1),
        (reduce_start, 0, 0), (reduce_step, 1, 0, 1), (gather, 1, 3), (gather, 0, 1), (gather, 0, 2),
        (reduce_start, 1, 3), (reduce_start, 0, 1), (reduce_start, 0, 2), (reduce_step, 1, 1, 1),
        (reduce_step, 1, 2, 1), (reduce_step, 0, 0, 1), (gather, 0, 3), (reduce_step, 1, 0, 2),
        (reduce_start, 0, 3), (reduce_step, 1, 3, 1), (reduce_step, 0, 1, 1), (reduce_step, 0, 2, 1),
        (attend_some, 1), (reduce_step, 1, 1, 2), (reduce_step, 1, 2, 2), (reduce_step, 0, 0, 2),
        (reduce_step, 0, 3, 1), (attend_some, 2), (reduce_step, 1, 0, 3), (reduce_step, 1, 3, 2),
        (reduce_step, 0, 1, 2), (reduce_step, 0, 2, 2), (attend_some, 2), (reduce_step, 1, 1, 3),
        (reduce_step, 1, 2, 3), (reduce_step, 0, 0, 3), (reduce_step, 0, 3, 2), (attend_some, 2),
        (reduce_step, 1, 3, 3), (reduce_step, 0, 1, 3), (reduce_step, 0, 2, 3), (attend_some, 1), (activate, 0),
        (reduce_step, 0, 3, 3), (activate, 1), (activate, 2), (attend_some, 1), (activate, 3), (attend_some, 1),
        (forward, 0, 0, 1), (forward, 0, 1, 1), (forward, 0, 2, 1), (forward, 0, 3, 1), (attend_some, 2),
        (forward, 0, 0, 2), (forward, 0, 1, 2), (forward, 0, 2, 2), (forward, 0, 3, 2), (spread_out, 1, 0),
        (spread_out, 1, 1), (spread_out, 1, 2), (spread_out, 1, 3), (attend_some, 2), (forward, 0, 0, 3),
        (forward, 0, 1, 3), (forward, 0, 2, 3), (forward, 0, 3, 3), (attend_some, 1), (forward, 1, 0, 1),
        (forward, 1, 1, 1), (forward, 1, 2, 1), (forward, 1, 3, 1), (input_gradient, 0), (input_gradient, 1),
        (input_gradient, 2), (input_gradient, 3), (attend_some, 1), (give_back, 0), (give_back, 1),
        (give_back, 2), (give_back, 3), (weight_gradient, 0, 0), (weight_gradient, 0, 1), (weight_gradient, 0, 2),
        (weight_gradient, 0, 3), (forward, 1, 0, 2), (forward, 1, 1, 2), (forward, 1, 2, 2), (forward, 1, 3, 2),
        (attend_some, 1), (sum_y,), (hand_over, 0), (forward, 1, 0, 3), (forward, 1, 1, 3), (forward, 1, 2, 3),
        (forward, 1, 3, 3), (sum_x,), (whole, 1, 0), (weight_gradient, 1, 0), (whole, 1, 1),
        (weight_gradient, 1, 1), (whole, 1, 2), (weight_gradient, 1, 2), (whole, 1, 3), (weight_gradient, 1, 3),
        (hand_over, 1),
    ]
    for step, *which in plan:
        step(*which)
    attend_some(PAIRS)
    for s in range(1, 8):
        arrived(hrecv.at[(z + 8 - s) % 8], h_send.at[s - 1], h_recv.at[s - 1], z_peer(s))

    def piece(n):
        return hrecv[n % 8].astype(F32)[(n // 8) * 8 : (n // 8) * 8 + 8]

    inverse = 1.0 / root_mean
    projection = jnp.zeros((8, 256), F32)
    for n, cols in enumerate(groups):
        projection = projection + piece(n) * (state[:, cols] * inverse)
    projection = jnp.sum(projection, axis=1, keepdims=True) / D
    sel_t = t_dot(sel_b, (iota((8, 128), 0) == iota((8, 128), 1)).astype(BF16))[:, 0:8].astype(BF16)
    spreads = []
    for n, cols in enumerate(groups):
        normed = state[:, cols] * inverse
        grad = (dlo[:, cols] + (piece(n) - normed * projection) * inverse) * occupied
        spreads.append(spread(grad))
    p = prob[...]
    pb = p.astype(BF16)
    dp = jnp.concatenate([dot_t(spreads[n], v[:, cols]) for n, cols in enumerate(groups)], axis=0)
    delta = jnp.sum(pb.astype(F32) * dp, axis=1, keepdims=True)
    sg = (p * (dp - delta)).astype(BF16)
    for n, cols in enumerate(groups):
        mine = slice(n * 32, n * 32 + 32)
        q_grad = (fold(dot(sg[mine], k[:, cols])) * SCALE).astype(BF16)
        dq[:, cols] = dq[:, cols] + dot(sel_t, q_grad).astype(BF16)
        dko[:, cols] = (dkb[:, cols] + t_dot(sg[mine], spread(qr[:, cols]))).astype(BF16)
        dvo[:, cols] = (dvb[:, cols] + t_dot(pb[mine], spreads[n])).astype(BF16)

    for copy in outs:
        copy.wait()
    arrived(gu_hbm.at[:, other_cols], o_send.at[0], o_recv.at[0], pair_peer)
    arrived(gd_hbm.at[:, other_cols], o_send.at[1], o_recv.at[1], pair_peer)
    for copy in sent:
        copy.wait_send()


def write_out(*refs):
    sems = refs[10]
    copies = [pltpu.make_async_copy(refs[n], refs[5 + n], sems.at[n]) for n in range(5)]
    for copy in copies:
        copy.start()
    for copy in copies:
        copy.wait()


def local(query, key, value, resid, d_out, routes, gates, w_up, w_down):
    hbm = pl.BlockSpec(memory_space=pl.ANY)
    pinned = pl.BlockSpec(memory_space=pltpu.HBM)
    vmem = pl.BlockSpec(memory_space=pltpu.VMEM)
    rows = (128, D)
    vm = pltpu.VMEM
    dma = pltpu.SemaphoreType.DMA
    results = pl.pallas_call(
        kernel,
        out_shape=(
            jax.ShapeDtypeStruct(rows, BF16),
            jax.ShapeDtypeStruct(rows, BF16),
            jax.ShapeDtypeStruct(rows, BF16),
            jax.ShapeDtypeStruct((256, 1024), BF16),
            jax.ShapeDtypeStruct((256, 1024), BF16),
        ),
        in_specs=[vmem, vmem] + [hbm] * 5 + [pinned] * 2,
        out_specs=(vmem,) * 3 + (hbm,) * 2,
        scratch_shapes=[
            vm(rows, BF16), vm(rows, BF16), vm(rows, BF16), vm(rows, BF16), vm(rows, BF16),
            vm((2, 256, 512), BF16), vm((2, 256, 512), BF16), vm((2, 256, 512), BF16), vm((128, 128), BF16),
            vm((8, D), F32), vm((8, D), F32), vm((8, D), F32), vm((512, 128), F32),
            vm((2, 8, 16, 256), BF16), vm((2, 8, 16, 256), BF16), vm((2, 4, 2, 4, 2, 32, 256), BF16),
            vm((2, 4, 8, 32, 512), BF16), vm((2, 2, 4, 4, 32, 512), BF16),
            vm((2, 4, 8, 32, 512), BF16),
            vm((2, 256, 512), F32), vm((2, 256, 512), F32), vm((2, 256, 512), BF16), vm((2, 256, 512), BF16),
            vm((4, 2, 128, 512), BF16), vm((4, 128, 512), BF16), vm((4, 128, 512), BF16), vm((3, 128, 512), BF16),
            vm((4, 32, 512), BF16), vm((3, 32, 512), BF16), vm((8, 16, 256), BF16), vm((8, 16, 256), BF16),
            vm(rows, F32), vm(rows, F32),
            dma((9,)), dma((2,)), dma((2, 4)), dma((2, 4)), dma((2, 7)), dma((2, 7)), dma((2, 3)), dma((2, 3)),
            dma((2, 4)), dma((2, 4)), dma((2, 4)), dma((2, 4)),
            dma((2, 2, 4, 4)), dma((2, 2, 4, 4)), dma((2, 4, 8)), dma((2, 4, 8)), dma((4,)), dma((4,)), dma((3,)), dma((3,)),
            dma((3,)), dma((3,)), dma((7,)), dma((7,)), dma((2,)), dma((2,)),
        ],
        compiler_params=pltpu.CompilerParams(
            collective_id=0, has_side_effects=True, vmem_limit_bytes=61180000
        ),
    )(routes.T, gates.T, query, key, value, resid, d_out, w_up, w_down)
    return pl.pallas_call(
        write_out,
        out_shape=tuple(jax.ShapeDtypeStruct(part.shape, part.dtype) for part in results),
        in_specs=[vmem] * 5,
        out_specs=(hbm,) * 5,
        scratch_shapes=[dma((5,))],
    )(*results)


def solution(mesh):
    tokens = P(("dp", "expert"), None)
    weights = P("dp", "expert")
    return jax.shard_map(
        local,
        mesh=mesh,
        in_specs=(tokens,) * 7 + (weights,) * 2,
        out_specs=(tokens,) * 3 + (weights,) * 2,
        check_vma=False,
    )
```

```python
import functools

import jax
import jax.numpy as jnp
from jax import lax
from jax.experimental import pallas as pl
from jax.experimental.pallas import tpu as pltpu
from jax.sharding import PartitionSpec as P

MESH = pl.DeviceIdType.MESH
F32 = jnp.float32
BF16 = jnp.bfloat16
D = 4096
SCALE = 0.125
EPS = 1e-06
Y_OFFSETS = (0, 1, 3, 2)
PAIRS = 32


def dot(a, b):
    return lax.dot_general(a, b, (((1,), (0,)), ((), ())), preferred_element_type=F32)


def dot_t(a, b):
    return lax.dot_general(a, b, (((1,), (1,)), ((), ())), preferred_element_type=F32)


def t_dot(a, b):
    return lax.dot_general(a, b, (((0,), (0,)), ((), ())), preferred_element_type=F32)


def iota(shape, dim):
    return lax.broadcasted_iota(jnp.int32, shape, dim)


def kernel(
    routes_ref, gates_ref, q_hbm, k_hbm, v_hbm, r_hbm, d_hbm, wu_hbm, wd_hbm,
    dq, dko, dvo, gu_hbm, gd_hbm,
    q, k, v, r, d, wu, wd, wx, keep, qr, dlo, state, prob,
    asend, arecv, g, part, rs, ag, gu_acc, gd_acc, gu_out, gd_out,
    rsend, rcore, rysend, ryrecv, rxsend, rxrecv, hsend, hrecv,
    dkb, dvb,
    load_sem, out_sem, w_send, w_recv, a_send, a_recv, x_send, x_recv, c_send, c_recv, y_send, y_recv,
    rs_send, rs_recv, ag_send, ag_recv, rc_send, rc_recv, ry_send, ry_recv, rx_send, rx_recv, h_send, h_recv,
    o_send, o_recv,
):
    i = lax.axis_index("dp")
    j = lax.axis_index("expert")
    xl = i // 8
    z = i % 8
    y = j // 4
    xh = (j // 2) % 2
    c = j % 2
    x = xh * 2 + xl

    def dev(x_to, y_to, z_to, c_to):
        return ((x_to % 2) * 8 + z_to, y_to * 4 + (x_to // 2) * 2 + c_to)

    def z_peer(step):
        return dev(x, y, (z + step) % 8, c)

    def x_peer(step):
        return dev((x + step) % 4, y, z, c)

    def y_peer(step):
        return dev(x, (y + step) % 4, z, c)

    core_peer = dev(x, y, z, 1 - c)
    pair_peer = (((1 - xl) * 8 + z), j)

    barrier = pltpu.get_barrier_semaphore()
    peers = [z_peer(s) for s in range(1, 8)] + [x_peer(s) for s in range(1, 4)]
    peers += [y_peer(s) for s in range(1, 4)] + [core_peer]
    for peer in peers:
        pl.semaphore_signal(barrier, inc=1, device_id=peer, device_id_type=MESH)

    loads = []
    for n, (src, dst) in enumerate(((d_hbm, d), (q_hbm, q), (k_hbm, k), (r_hbm, r), (v_hbm, v))):
        loads.append(pltpu.make_async_copy(src, dst, load_sem.at[n]))
    own_cols = pl.ds(pl.multiple_of(xl * 512, 512), 512)
    other_cols = pl.ds(pl.multiple_of((1 - xl) * 512, 512), 512)
    loads.append(pltpu.make_async_copy(wd_hbm.at[:, own_cols], wd.at[xl], load_sem.at[5]))
    loads.append(pltpu.make_async_copy(wu_hbm.at[:, own_cols], wu.at[xl], load_sem.at[6]))
    loads.append(pltpu.make_async_copy(wd_hbm.at[:, other_cols], wx.at[0], load_sem.at[7]))
    loads.append(pltpu.make_async_copy(wu_hbm.at[:, other_cols], wx.at[1], load_sem.at[8]))
    for copy in loads:
        copy.start()

    sent = []

    def send(src, dst, send_sem, recv_sem, peer):
        copy = pltpu.make_async_remote_copy(
            src_ref=src, dst_ref=dst, send_sem=send_sem, recv_sem=recv_sem, device_id=peer, device_id_type=MESH
        )
        copy.start()
        sent.append(copy)

    def arrived(dst, send_sem, recv_sem, peer):
        pltpu.make_async_remote_copy(
            src_ref=dst, dst_ref=dst, send_sem=send_sem, recv_sem=recv_sem, device_id=peer, device_id_type=MESH
        ).wait_recv()

    flags = (routes_ref[...] == 0).astype(F32)
    picked = gates_ref[...] * flags
    gate_row = picked[0:1, :] + picked[1:2, :]
    hit = jnp.maximum(flags[0:1, :], flags[1:2, :])
    upper = (iota((128, 128), 0) <= iota((128, 128), 1)).astype(BF16)
    hits = jnp.broadcast_to(hit, (8, 128))
    rank = dot(hits.astype(BF16), upper) - 1.0
    slot = iota((8, 128), 0).astype(F32)
    sel = jnp.where((rank == slot) & (slot < 4.0), hits, 0.0)
    occupied = jnp.sum(sel, axis=1, keepdims=True)
    position = jnp.sum(sel * iota((8, 128), 1).astype(F32), axis=1, keepdims=True)
    gate = jnp.sum(sel * gate_row, axis=1, keepdims=True)
    sel_b = sel.astype(BF16)
    keep[...] = (1.0 - t_dot(sel_b, jnp.ones((8, 128), BF16))).astype(BF16)
    seen = iota((8, 128), 1).astype(F32) <= position
    seen32 = jnp.concatenate([seen] * 4, axis=0)
    lane_head = iota((8, 256), 1) // 64

    def spread(rows):
        return jnp.concatenate([jnp.where(lane_head == h, rows, 0.0) for h in range(4)], axis=0).astype(BF16)

    def fold(rows):
        total = jnp.where(lane_head == 0, rows[0:8], 0.0)
        for h in range(1, 4):
            total = total + jnp.where(lane_head == h, rows[8 * h : 8 * h + 8], 0.0)
        return total

    groups = [slice(n * 256, n * 256 + 256) for n in range(16)]
    loads[0].wait()
    for cols in groups:
        dlo[:, cols] = dot(sel_b, d[:, cols])
    for n in range(8):
        both = [gate * dlo[:, groups[n]], gate * dlo[:, groups[8 + n]]]
        asend[1, n] = jnp.concatenate(both, axis=0).astype(BF16)

    loads[1].wait()
    loads[2].wait()
    for cols in groups:
        qr[:, cols] = dot(sel_b, q[:, cols]) * SCALE
    scores = jnp.concatenate([dot_t(spread(qr[:, cols]), k[:, cols]) for cols in groups], axis=0)
    scores = jnp.where(jnp.concatenate([seen32] * 16, axis=0), scores, -jnp.inf)
    weights = jnp.exp(scores - jnp.max(scores, axis=1, keepdims=True))
    prob[...] = weights / jnp.sum(weights, axis=1, keepdims=True)

    pl.semaphore_wait(barrier, len(peers))

    def to_blocks(m):
        for s in range(1, 8):
            send(asend.at[m, (z + s) % 8], arecv.at[m, z], a_send.at[m, s - 1], a_recv.at[m, s - 1], z_peer(s))
        arecv[m, z] = asend[m, z]

    def send_weights(n):
        dst = (wd, wu)[n]
        loads[7 + n].wait()
        for part_n in range(4):
            rows = slice(part_n * 64, part_n * 64 + 64)
            send(
                wx.at[n, rows], dst.at[xl, rows], w_send.at[n, part_n], w_recv.at[n, part_n], pair_peer
            )

    def weights_here(n):
        loads[5 + n].wait()
        dst = (wd, wu)[n]
        for part_n in range(4):
            rows = slice(part_n * 64, part_n * 64 + 64)
            arrived(dst.at[1 - xl, rows], w_send.at[n, part_n], w_recv.at[n, part_n], pair_peer)

    send_weights(0)
    to_blocks(1)

    loads[3].wait()
    loads[4].wait()
    for cols in groups:
        state[:, cols] = dot(sel_b, r[:, cols])
    squares = jnp.zeros((8, 256), F32)
    for n, cols in enumerate(groups):
        st = state[:, cols] + fold(dot(prob[n * 32 : n * 32 + 32, :].astype(BF16), v[:, cols]))
        state[:, cols] = st
        squares = squares + st * st
    squares = jnp.sum(squares, axis=1, keepdims=True)
    root_mean = jnp.sqrt(squares / D + EPS)
    for n in range(8):
        both = [state[:, groups[m]] / root_mean * occupied for m in (n, 8 + n)]
        asend[0, n] = jnp.concatenate(both, axis=0).astype(BF16)
    to_blocks(0)

    lane0 = iota((128, 128), 1) < 64
    causal = iota((256, 128), 0) % 128 >= iota((256, 128), 1)

    def two(rows):
        zero = jnp.zeros_like(rows)
        return jnp.concatenate([jnp.where(lane0, rows, zero), jnp.where(lane0, zero, rows)], axis=0)

    def attend(n, carry):
        cols = pl.ds(pl.multiple_of(n * 128, 128), 128)
        k2 = k[:, cols]
        qs = two(q[:, cols] * jnp.asarray(SCALE, BF16))
        scores = jnp.where(causal, dot_t(qs, k2), -jnp.inf)
        weights = jnp.exp(scores - jnp.max(scores, axis=1, keepdims=True))
        p = weights / jnp.sum(weights, axis=1, keepdims=True)
        pb = p.astype(BF16)
        ds = two(d[:, cols] * keep[...])
        dp = dot_t(ds, v[:, cols])
        delta = jnp.sum(pb.astype(F32) * dp, axis=1, keepdims=True)
        sg = (p * (dp - delta)).astype(BF16)
        dkb[:, cols] = t_dot(sg, qs)
        dvb[:, cols] = t_dot(pb, ds)
        sides = jnp.concatenate([sg[:128], sg[128:]], axis=1)
        dq[:, cols] = (dot(sides, two(k2)) * SCALE).astype(BF16)
        return carry

    done_pairs = [0]

    def attend_some(count):
        first = done_pairs[0]
        last = min(PAIRS, first + count)
        if last > first:
            lax.fori_loop(first, last, attend, 0)
        done_pairs[0] = last

    row = iota((64, 128), 0)
    col = iota((64, 128), 1)
    permute = (row // 32 == (col // 8) % 2) & ((row % 32) // 4 == col // 16) & (row % 4 == col % 8)
    permute = permute.astype(BF16)

    def gather_x(m):
        for s in range(1, 8):
            arrived(arecv.at[m, (z + 8 - s) % 8], a_send.at[m, s - 1], a_recv.at[m, s - 1], z_peer(s))
        tiles = dot(permute, arecv[m].reshape(128, 256)).astype(BF16)
        block = g.at[m, y, c, x]
        block[...] = tiles.reshape(2, 32, 256)
        for s in range(1, 4):
            send(block, block, x_send.at[m, s - 1], x_recv.at[m, s - 1], x_peer(s))

    def gather_y(m):
        for s in range(1, 4):
            arrived(g.at[m, y, c, (x + 4 - s) % 4], x_send.at[m, s - 1], x_recv.at[m, s - 1], x_peer(s))
        block = g.at[m, y, c]
        send(block, block, c_send.at[m, 0], c_recv.at[m, 0], core_peer)
        send(block, block, y_send.at[m, 0], y_recv.at[m, 0], y_peer(3))
        send(block, block, y_send.at[m, 1], y_recv.at[m, 1], y_peer(1))

    def y_of(w):
        return (y + Y_OFFSETS[w]) % 4

    def rows_of(w, f, m):
        return g[m, y_of(w), :, :, f].reshape(256, 256)

    x_low = slice(0, 2)
    x_high = slice(2, 4)

    def gather(m, w):
        block = g.at[m, y_of(w), c]
        if w == 1:
            arrived(block, y_send.at[m, 0], y_recv.at[m, 0], y_peer(3))
            send(block.at[x_low], block.at[x_low], y_send.at[m, 2], y_recv.at[m, 2], y_peer(3))
        if w == 2:
            arrived(block, y_send.at[m, 1], y_recv.at[m, 1], y_peer(1))
            send(block.at[x_high], block.at[x_high], y_send.at[m, 3], y_recv.at[m, 3], y_peer(1))
        if w == 3:
            arrived(block.at[x_low], y_send.at[m, 2], y_recv.at[m, 2], y_peer(3))
            arrived(block.at[x_high], y_send.at[m, 3], y_recv.at[m, 3], y_peer(1))
        send(block, block, c_send.at[m, w], c_recv.at[m, w], core_peer)

    up_half = slice(0, 16)
    down_half = slice(16, 32)

    def reduce_start(m, w):
        arrived(g.at[m, y_of(w), 1 - c], c_send.at[m, w], c_recv.at[m, w], core_peer)
        right = (wu, wd)[m]
        terms = dot(rows_of(w, 0, m), right[0]) + dot(rows_of(w, 1, m), right[1])
        part[m, w] = terms.astype(BF16).reshape(8, 32, 512)
        far = part.at[m, w, (z + 4) % 8]
        ups, downs = rs.at[m, 0, w, 0], rs.at[m, 1, w, 0]
        send(far.at[up_half], ups.at[up_half], rs_send.at[m, 0, w, 0], rs_recv.at[m, 0, w, 0], z_peer(1))
        send(far.at[down_half], downs.at[down_half], rs_send.at[m, 1, w, 0], rs_recv.at[m, 1, w, 0], z_peer(7))

    def reduce_step(m, w, s):
        for side in range(2):
            block = (z + 4 - s) % 8 if side == 0 else (z + 4 + s) % 8
            here, fresh = (up_half, down_half) if side == 0 else (down_half, up_half)
            peer = z_peer(1) if side == 0 else z_peer(7)
            last = rs.at[m, side, w, s - 1]
            sems = rs_send.at[m, side, w, s - 1], rs_recv.at[m, side, w, s - 1]
            if s == 1:
                arrived(last.at[here], *sems, peer)
                last[here] = (last[here].astype(F32) + part[m, w, block, here].astype(F32)).astype(BF16)
                last[fresh] = part[m, w, block, fresh]
            else:
                arrived(last, *sems, peer)
                last[...] = (last[...].astype(F32) + part[m, w, block].astype(F32)).astype(BF16)
            send(last, rs.at[m, side, w, s], rs_send.at[m, side, w, s], rs_recv.at[m, side, w, s], peer)

    def reduced(m, w):
        total = part[m, w, z].astype(F32)
        for side in range(2):
            last = rs.at[m, side, w, 3]
            peer = z_peer(1) if side == 0 else z_peer(7)
            arrived(last, rs_send.at[m, side, w, 3], rs_recv.at[m, side, w, 3], peer)
            total = total + last[...].astype(F32)
        return total

    def activate(w):
        back = reduced(1, w)
        h = reduced(0, w)
        root = 0.7978845608028654
        inner = jnp.tanh(root * (h + 0.044715 * (h * h * h)))
        half = 0.5 * (1.0 + inner)
        slope = half + 0.5 * h * (1.0 - inner * inner) * (root * (1.0 + 3.0 * 0.044715 * (h * h)))
        ag[0, w, z] = (back * slope).astype(BF16)
        ag[1, w, z] = (h * half).astype(BF16)
        spread_out(0, w)

    def spread_out(m, w):
        send(ag.at[m, w, z], ag.at[m, w, z], ag_send.at[m, w, 0], ag_recv.at[m, w, 0], z_peer(1))
        send(ag.at[m, w, z], ag.at[m, w, z], ag_send.at[m, w, 4], ag_recv.at[m, w, 4], z_peer(7))

    def forward(m, w, s):
        up = (z + 8 - s) % 8
        down = (z + s) % 8
        block = ag.at[m, w, up]
        arrived(block, ag_send.at[m, w, s - 1], ag_recv.at[m, w, s - 1], z_peer(1))
        block = block.at[up_half] if s == 3 else block
        send(block, block, ag_send.at[m, w, s], ag_recv.at[m, w, s], z_peer(1))
        block = ag.at[m, w, down]
        arrived(block, ag_send.at[m, w, 3 + s], ag_recv.at[m, w, 3 + s], z_peer(7))
        block = block.at[down_half] if s == 3 else block
        send(block, block, ag_send.at[m, w, 4 + s], ag_recv.at[m, w, 4 + s], z_peer(7))

    def whole(m, w):
        far = (z + 4) % 8
        arrived(ag.at[m, w, far, up_half], ag_send.at[m, w, 3], ag_recv.at[m, w, 3], z_peer(1))
        arrived(ag.at[m, w, far, down_half], ag_send.at[m, w, 7], ag_recv.at[m, w, 7], z_peer(7))

    def input_gradient(w):
        whole(0, w)
        hidden_grad = ag[0, w].reshape(256, 512)
        for f in range(2):
            back = dot_t(hidden_grad, wu[f]).astype(BF16)
            rsend[w, :, :, f * 256 : f * 256 + 256] = back.reshape(2, 128, 256)
        send(rsend.at[w, 1 - c], rcore.at[w], rc_send.at[w], rc_recv.at[w], core_peer)

    def weight_gradient(m, w):
        acc, out = ((gu_acc, gu_out), (gd_acc, gd_out))[m]
        right = ag[m, w].reshape(256, 512)
        for f in range(2):
            term = t_dot(rows_of(w, f, m), right)
            if w == 0:
                acc[f] = term
            elif w < 3:
                acc[f] += term
            else:
                out[f] = (acc[f] + term).astype(BF16)

    def give_back(w):
        arrived(rcore.at[w], rc_send.at[w], rc_recv.at[w], core_peer)
        total = rsend[w, c].astype(F32) + rcore[w].astype(F32)
        rysend[w] = total.astype(BF16)
        if w > 0:
            send(rysend.at[w], ryrecv.at[w - 1], ry_send.at[w - 1], ry_recv.at[w - 1], y_peer(Y_OFFSETS[w]))

    def sum_y():
        total = rysend[0].astype(F32)
        for w in range(1, 4):
            arrived(ryrecv.at[w - 1], ry_send.at[w - 1], ry_recv.at[w - 1], y_peer(1))
            total = total + ryrecv[w - 1].astype(F32)
        rxsend[...] = total.astype(BF16).reshape(4, 32, 512)
        for s in range(1, 4):
            send(rxsend.at[(x + s) % 4], rxrecv.at[s - 1], rx_send.at[s - 1], rx_recv.at[s - 1], x_peer(s))

    def sum_x():
        returned = rxsend[x].astype(F32)
        for s in range(1, 4):
            arrived(rxrecv.at[s - 1], rx_send.at[s - 1], rx_recv.at[s - 1], x_peer(s))
            returned = returned + rxrecv[s - 1].astype(F32)
        returned = returned.astype(BF16)
        row32 = iota((128, 32), 0)
        col32 = iota((128, 32), 1)
        placed = (row32 // 16 == col32 // 4) & (row32 % 8 == col32 % 4)
        first = (placed & ((row32 // 8) % 2 == 0)).astype(BF16)
        second = (placed & ((row32 // 8) % 2 == 1)).astype(BF16)
        homes = dot(first, returned[:, 0:256]) + dot(second, returned[:, 256:512])
        hsend[...] = homes.astype(BF16).reshape(8, 16, 256)
        for s in range(1, 8):
            send(hsend.at[(z + s) % 8], hrecv.at[z], h_send.at[s - 1], h_recv.at[s - 1], z_peer(s))
        hrecv[z] = hsend[z]

    outs = []

    def hand_over(m):
        out, whole_out = ((gu_out, gu_hbm), (gd_out, gd_hbm))[m]
        send(out.at[1 - xl], whole_out.at[:, own_cols], o_send.at[m], o_recv.at[m], pair_peer)
        copy = pltpu.make_async_copy(out.at[xl], whole_out.at[:, own_cols], out_sem.at[m])
        copy.start()
        outs.append(copy)

    plan = [
        (attend_some, 2), (gather_x, 1), (attend_some, 4), (gather_x, 0), (send_weights, 1), (gather_y, 1),
        (attend_some, 1), (weights_here, 0), (reduce_start, 1, 0), (attend_some, 2), (gather_y, 0),
        (gather, 1, 1), (gather, 1, 2), (reduce_start, 1, 1), (reduce_start, 1, 2), (weights_here, 1),
        (reduce_start, 0, 0), (reduce_step, 1, 0, 1), (gather, 1, 3), (gather, 0, 1), (gather, 0, 2),
        (reduce_start, 1, 3), (reduce_start, 0, 1), (reduce_start, 0, 2), (reduce_step, 1, 1, 1),
        (reduce_step, 1, 2, 1), (reduce_step, 0, 0, 1), (gather, 0, 3), (reduce_step, 1, 0, 2),
        (reduce_start, 0, 3), (reduce_step, 1, 3, 1), (reduce_step, 0, 1, 1), (reduce_step, 0, 2, 1),
        (attend_some, 1), (reduce_step, 1, 1, 2), (reduce_step, 1, 2, 2), (reduce_step, 0, 0, 2),
        (reduce_step, 0, 3, 1), (attend_some, 2), (reduce_step, 1, 0, 3), (reduce_step, 1, 3, 2),
        (reduce_step, 0, 1, 2), (reduce_step, 0, 2, 2), (attend_some, 2), (reduce_step, 1, 1, 3),
        (reduce_step, 1, 2, 3), (reduce_step, 0, 0, 3), (reduce_step, 0, 3, 2), (attend_some, 2),
        (reduce_step, 1, 3, 3), (reduce_step, 0, 1, 3), (reduce_step, 0, 2, 3), (attend_some, 1), (activate, 0),
        (reduce_step, 0, 3, 3), (activate, 1), (activate, 2), (attend_some, 1), (activate, 3), (attend_some, 1),
        (forward, 0, 0, 1), (forward, 0, 1, 1), (forward, 0, 2, 1), (forward, 0, 3, 1), (attend_some, 2),
        (forward, 0, 0, 2), (forward, 0, 1, 2), (forward, 0, 2, 2), (forward, 0, 3, 2), (spread_out, 1, 0),
        (spread_out, 1, 1), (spread_out, 1, 2), (spread_out, 1, 3), (attend_some, 2), (forward, 0, 0, 3),
        (forward, 0, 1, 3), (forward, 0, 2, 3), (forward, 0, 3, 3), (attend_some, 1), (forward, 1, 0, 1),
        (forward, 1, 1, 1), (forward, 1, 2, 1), (forward, 1, 3, 1), (input_gradient, 0), (input_gradient, 1),
        (input_gradient, 2), (input_gradient, 3), (attend_some, 1), (give_back, 0), (give_back, 1),
        (give_back, 2), (give_back, 3), (weight_gradient, 0, 0), (weight_gradient, 0, 1), (weight_gradient, 0, 2),
        (weight_gradient, 0, 3), (forward, 1, 0, 2), (forward, 1, 1, 2), (forward, 1, 2, 2), (forward, 1, 3, 2),
        (attend_some, 1), (sum_y,), (hand_over, 0), (forward, 1, 0, 3), (forward, 1, 1, 3), (forward, 1, 2, 3),
        (forward, 1, 3, 3), (sum_x,), (whole, 1, 0), (weight_gradient, 1, 0), (whole, 1, 1),
        (weight_gradient, 1, 1), (whole, 1, 2), (weight_gradient, 1, 2), (whole, 1, 3), (weight_gradient, 1, 3),
        (hand_over, 1),
    ]
    for step, *which in plan:
        step(*which)
    attend_some(PAIRS)
    for s in range(1, 8):
        arrived(hrecv.at[(z + 8 - s) % 8], h_send.at[s - 1], h_recv.at[s - 1], z_peer(s))

    def piece(n):
        return hrecv[n % 8].astype(F32)[(n // 8) * 8 : (n // 8) * 8 + 8]

    inverse = 1.0 / root_mean
    projection = jnp.zeros((8, 256), F32)
    for n, cols in enumerate(groups):
        projection = projection + piece(n) * (state[:, cols] * inverse)
    projection = jnp.sum(projection, axis=1, keepdims=True) / D
    sel_t = t_dot(sel_b, (iota((8, 128), 0) == iota((8, 128), 1)).astype(BF16))[:, 0:8].astype(BF16)
    spreads = []
    for n, cols in enumerate(groups):
        normed = state[:, cols] * inverse
        grad = (dlo[:, cols] + (piece(n) - normed * projection) * inverse) * occupied
        spreads.append(spread(grad))
    p = prob[...]
    pb = p.astype(BF16)
    dp = jnp.concatenate([dot_t(spreads[n], v[:, cols]) for n, cols in enumerate(groups)], axis=0)
    delta = jnp.sum(pb.astype(F32) * dp, axis=1, keepdims=True)
    sg = (p * (dp - delta)).astype(BF16)
    for n, cols in enumerate(groups):
        mine = slice(n * 32, n * 32 + 32)
        q_grad = (fold(dot(sg[mine], k[:, cols])) * SCALE).astype(BF16)
        dq[:, cols] = dq[:, cols] + dot(sel_t, q_grad).astype(BF16)
        dko[:, cols] = (dkb[:, cols] + t_dot(sg[mine], spread(qr[:, cols]))).astype(BF16)
        dvo[:, cols] = (dvb[:, cols] + t_dot(pb[mine], spreads[n])).astype(BF16)

    for copy in outs:
        copy.wait()
    arrived(gu_hbm.at[:, other_cols], o_send.at[0], o_recv.at[0], pair_peer)
    arrived(gd_hbm.at[:, other_cols], o_send.at[1], o_recv.at[1], pair_peer)
    for copy in sent:
        copy.wait_send()


def write_out(*refs):
    sources, results, held = refs[0:5], refs[5:10], refs[10:15]
    read_sem, write_sem = refs[15:17]
    reads, writes = [], []
    for n in range(5):
        half = sources[n].shape[0] // 2
        for part_n in range(2):
            rows = slice(part_n * half, part_n * half + half)
            kept = held[n].at[rows]
            reads.append(pltpu.make_async_copy(sources[n].at[rows], kept, read_sem.at[n, part_n]))
            writes.append(pltpu.make_async_copy(kept, results[n].at[rows], write_sem.at[n, part_n]))
    for copy in reads:
        copy.start()
    for read, write in zip(reads, writes):
        read.wait()
        write.start()
    for copy in writes:
        copy.wait()


def local(query, key, value, resid, d_out, routes, gates, w_up, w_down):
    hbm = pl.BlockSpec(memory_space=pl.ANY)
    pinned = pl.BlockSpec(memory_space=pltpu.HBM)
    vmem = pl.BlockSpec(memory_space=pltpu.VMEM)
    rows = (128, D)
    vm = pltpu.VMEM
    dma = pltpu.SemaphoreType.DMA
    results = pl.pallas_call(
        kernel,
        out_shape=(
            jax.ShapeDtypeStruct(rows, BF16),
            jax.ShapeDtypeStruct(rows, BF16),
            jax.ShapeDtypeStruct(rows, BF16),
            jax.ShapeDtypeStruct((256, 1024), BF16),
            jax.ShapeDtypeStruct((256, 1024), BF16),
        ),
        in_specs=[vmem, vmem] + [hbm] * 5 + [pinned] * 2,
        out_specs=(vmem,) * 3 + (hbm,) * 2,
        scratch_shapes=[
            vm(rows, BF16), vm(rows, BF16), vm(rows, BF16), vm(rows, BF16), vm(rows, BF16),
            vm((2, 256, 512), BF16), vm((2, 256, 512), BF16), vm((2, 256, 512), BF16), vm((128, 128), BF16),
            vm((8, D), F32), vm((8, D), F32), vm((8, D), F32), vm((512, 128), F32),
            vm((2, 8, 16, 256), BF16), vm((2, 8, 16, 256), BF16), vm((2, 4, 2, 4, 2, 32, 256), BF16),
            vm((2, 4, 8, 32, 512), BF16), vm((2, 2, 4, 4, 32, 512), BF16),
            vm((2, 4, 8, 32, 512), BF16),
            vm((2, 256, 512), F32), vm((2, 256, 512), F32), vm((2, 256, 512), BF16), vm((2, 256, 512), BF16),
            vm((4, 2, 128, 512), BF16), vm((4, 128, 512), BF16), vm((4, 128, 512), BF16), vm((3, 128, 512), BF16),
            vm((4, 32, 512), BF16), vm((3, 32, 512), BF16), vm((8, 16, 256), BF16), vm((8, 16, 256), BF16),
            vm(rows, F32), vm(rows, F32),
            dma((9,)), dma((2,)), dma((2, 4)), dma((2, 4)), dma((2, 7)), dma((2, 7)), dma((2, 3)), dma((2, 3)),
            dma((2, 4)), dma((2, 4)), dma((2, 4)), dma((2, 4)),
            dma((2, 2, 4, 4)), dma((2, 2, 4, 4)), dma((2, 4, 8)), dma((2, 4, 8)), dma((4,)), dma((4,)), dma((3,)), dma((3,)),
            dma((3,)), dma((3,)), dma((7,)), dma((7,)), dma((2,)), dma((2,)),
        ],
        compiler_params=pltpu.CompilerParams(
            collective_id=0, has_side_effects=True, vmem_limit_bytes=61180000
        ),
    )(routes.T, gates.T, query, key, value, resid, d_out, w_up, w_down)
    return pl.pallas_call(
        write_out,
        out_shape=tuple(jax.ShapeDtypeStruct(part.shape, part.dtype) for part in results),
        in_specs=[hbm] * 5,
        out_specs=(hbm,) * 5,
        scratch_shapes=[vm(part.shape, part.dtype) for part in results] + [dma((5, 2)), dma((5, 2))],
    )(*results)


def solution(mesh):
    tokens = P(("dp", "expert"), None)
    weights = P("dp", "expert")
    return jax.shard_map(
        local,
        mesh=mesh,
        in_specs=(tokens,) * 7 + (weights,) * 2,
        out_specs=(tokens,) * 3 + (weights,) * 2,
        check_vma=False,
    )
```
